512 devices in a mesh: sec: 32 (over y, x, core), cross: 16 (over z).
Axes of the slice: x: 4, y: 4, z: 16, core: 2. Of those that a mesh axis runs over, the one named last changes fastest.
Arguments:
- state: float32 [5, 1024, 4, 4096], P(None, 'sec', None, 'cross'), may hold values from -1.1 to 5, as said below
- time_step: float32 [1024, 4, 4096], P('sec', None, 'cross'), may hold values from 0.001 to 0.01
- to_char: float32 [5, 5], replicated, may hold values from -2.5 to 2.5
- to_cons: float32 [5, 5], replicated, may hold values from -2.5 to 2.5
- lower_bands: float32 [3, 3, 1024], P(None, None, 'sec'), may hold values from -1.9 to 1.25, as said below
- upper_bands: float32 [3, 2, 1024], P(None, None, 'sec'), may hold values from -1.5 to 0.5, as said below
Outputs:
- update: float32 [5, 1024, 4, 4096], P(None, 'sec', None, 'cross')
The draws below stay inside these ranges and needn't reach their ends.
Inputs may be any that keep to these rules, and one draw needn't show every extreme that they name: `state`: density lies in 0.7 to 1.3, velocities within 0.8 in magnitude and pressure in 0.6 to 1.4; the energy follows from an ideal gas with ratio of heats 1.4. `lower_bands`: each lower factor has diagonal 0.8 to 1.25 and equals the diagonal times (1 - a S)(1 - b S) for a shift S, with 0 < a < 1 and 0.1 <= b <= 0.5 per cell. `upper_bands`: each upper factor equals (1 - a S')(1 - b S') for the backward shift S', with 0 < a < 1 and 0.1 <= b <= 0.5 per cell.
All inputs are finite; a program needn't handle non-finite values.
Results may differ from the reference program's by a relative error of at most 0.0003.
Values sent between devices are 32-bit elements; how exact they have to be, the bound alone decides.
No kernel may reach another device: no remote copies, remote signals or barrier semaphores. Data moves between devices by JAX's collectives and lax.ppermute only.
A program may use at most 64 MiB of HBM per device.

```python
import math
import jax
import jax.numpy as jnp
from jax import lax

NL = 1024
NY = 4096


def root_pair(key, fast_share):
    stochastic_seeds = jax.random.split(key, 6)
    element_tally = NL
    slow = jax.random.uniform(stochastic_seeds[0], (3, 1), minval=0.2, maxval=2.0) / element_tally
    fast = jax.random.uniform(stochastic_seeds[1], (3, 1), minval=1.0 / 50.0, maxval=1.0 / 30.0)
    picked = jax.random.uniform(stochastic_seeds[2], (3, 1)) < fast_share
    traversal_throughput = jnp.where(picked, fast, slow) * jax.random.uniform(stochastic_seeds[3], (3, element_tally), minval=0.5, maxval=1.5)
    contiguous_span = jax.random.bernoulli(stochastic_seeds[4], 4.0 / element_tally, (3, element_tally))
    sluggish_multiplier = jnp.exp(-traversal_throughput) * jnp.where(contiguous_span, 0.6, 1.0)
    faster = jax.random.uniform(stochastic_seeds[5], (3, element_tally), minval=0.1, maxval=0.5)
    return (sluggish_multiplier, faster)


def draw_lower_bands(key, part):
    key = jax.random.fold_in(key, 11)
    share = 0.4
    sluggish_multiplier, faster = root_pair(key, share)
    diagonal = jax.random.uniform(jax.random.fold_in(key, 5), (3, NL), minval=0.8, maxval=1.25)
    return jnp.stack([sluggish_multiplier * faster * diagonal, -(sluggish_multiplier + faster) * diagonal, diagonal], axis=1).astype(jnp.float32)


def draw_upper_bands(key, part):
    key = jax.random.fold_in(key, 23)
    share = 0.4
    sluggish_multiplier, faster = root_pair(key, share)
    return jnp.stack([-(sluggish_multiplier + faster), sluggish_multiplier * faster], axis=1).astype(jnp.float32)


def draw_state(key, part):
    key = jax.random.fold_in(key, 37)
    stochastic_seeds = jax.random.split(key, 5)
    shape = (NL, 4, NY)
    density = jax.random.uniform(stochastic_seeds[0], shape, minval=0.7, maxval=1.3)
    speed_one = jax.random.uniform(stochastic_seeds[1], shape, minval=-0.5, maxval=0.5)
    speed_two = jax.random.uniform(stochastic_seeds[2], shape, minval=-0.5, maxval=0.5)
    speed_three = jax.random.uniform(stochastic_seeds[3], shape, minval=-0.5, maxval=0.5)
    pressure = jax.random.uniform(stochastic_seeds[4], shape, minval=0.6, maxval=1.4)
    energy = pressure / 0.4 + 0.5 * density * (speed_one * speed_one + speed_two * speed_two + speed_three * speed_three)
    return jnp.stack([density, density * speed_one, density * speed_two, density * speed_three, energy]).astype(jnp.float32)


def level_of(rng, dims, cuts, low, top_value):
    level = 1.0
    for dim, shards_of in cuts:
        steps = jax.random.uniform(jax.random.fold_in(jax.random.fold_in(rng, 6), dim), (shards_of,), jnp.float32, low / len(cuts), top_value / len(cuts))
        level = level * jnp.repeat(jnp.exp(steps), dims[dim] // shards_of).reshape((-1,) + (1,) * (len(dims) - 1 - dim))
    return level


def bell_draw(rng, dims, spread, reach, held_as=jnp.bfloat16):
    drawn = jax.random.normal(rng, dims, jnp.float32) * spread
    return jnp.minimum(jnp.maximum(drawn, -reach), reach).astype(held_as)


def setup_inputs(seed: int = 0) -> dict:
    splits = jax.random.split(jax.random.key(seed), 7)
    state = draw_state(jax.random.fold_in(splits[6], 71), 0)
    time_step = jnp.clip(jnp.exp(math.log(0.01) - 2.30258502 * jax.random.uniform(splits[1], (NL, 4, NY), jnp.float32) ** level_of(splits[1], (NL, 4, NY), ((0, 32), (2, 16)), -0.2, 0.2)), 0.001, 0.01)
    to_char = bell_draw(splits[2], (5, 5), 5 ** -0.5, 2.5, jnp.float32)
    to_cons = bell_draw(splits[3], (5, 5), 5 ** -0.5, 2.5, jnp.float32)
    lower_bands = draw_lower_bands(jax.random.fold_in(splits[6], 71), 0)
    upper_bands = draw_upper_bands(jax.random.fold_in(splits[6], 71), 0)
    return {"state": state, "time_step": time_step, "to_char": to_char, "to_cons": to_cons, "lower_bands": lower_bands, "upper_bands": upper_bands}


DISSIPATION = 0.0625
UPPER_LIMIT = lax.Precision.HIGHEST


def euler_flux(state, direction_axis):
    density = state[0]
    velocity = state[1 + direction_axis] / density
    kinetic = 0.5 * (state[1] * state[1] + state[2] * state[2] + state[3] * state[3]) / density
    pressure = 0.4 * (state[4] - kinetic)
    parts = [state[1 + direction_axis], state[1] * velocity, state[2] * velocity, state[3] * velocity, (state[4] + pressure) * velocity]
    parts[1 + direction_axis] = parts[1 + direction_axis] + pressure
    return jnp.stack(parts)


def reference(state, time_step, to_char, to_cons, lower_bands, upper_bands):
    numerical_transport_row = euler_flux(state, 0)
    line_pad = jnp.pad(numerical_transport_row, ((0, 0), (1, 1), (0, 0), (0, 0)))
    diff_line = 0.5 * (line_pad[:, 2:] - line_pad[:, :-2])
    state_pad = jnp.pad(state, ((0, 0), (2, 2), (0, 0), (0, 0)))
    fourth = state_pad[:, 4:] - 4.0 * state_pad[:, 3:-1] + 6.0 * state_pad[:, 2:-2] - 4.0 * state_pad[:, 1:-3] + state_pad[:, :-4]
    flux_side = euler_flux(state, 1)
    side_pad = jnp.pad(flux_side, ((0, 0), (0, 0), (0, 0), (1, 1)))
    diff_side = 0.5 * (side_pad[..., 2:] - side_pad[..., :-2])
    flux_third = euler_flux(state, 2)
    diff_third = 0.5 * (jnp.roll(flux_third, -1, axis=2) - jnp.roll(flux_third, 1, axis=2))
    residual = -(diff_line + diff_side + diff_third) - DISSIPATION * fourth
    right = time_step[None] * residual
    char = jnp.einsum('uv,vlzy->ulzy', to_char, right, precision=UPPER_LIMIT)
    system_of = jnp.array([0, 0, 0, 1, 2], jnp.int32)
    lower_var = jnp.take(lower_bands, system_of, axis=0).transpose(2, 0, 1)
    upper_var = jnp.take(upper_bands, system_of, axis=0).transpose(2, 0, 1)

    def forward_step(carry, inputs):
        prior_one, prior_two = carry
        values, coeffs = inputs
        result = (values - coeffs[:, 1, None, None] * prior_one - coeffs[:, 0, None, None] * prior_two) / coeffs[:, 2, None, None]
        return (result, prior_one), result

    zeros = jnp.zeros((5, state.shape[2], state.shape[3]), jnp.float32)
    _, forward = lax.scan(forward_step, (zeros, zeros), (char.transpose(1, 0, 2, 3), lower_var))

    def backward_step(carry, inputs):
        next_one, next_two = carry
        values, coeffs = inputs
        result = values - coeffs[:, 0, None, None] * next_one - coeffs[:, 1, None, None] * next_two
        return (result, next_one), result

    _, backward = lax.scan(backward_step, (zeros, zeros), (forward, upper_var), reverse=True)
    backward = backward.transpose(1, 0, 2, 3)
    return jnp.einsum('uv,vlzy->ulzy', to_cons, backward, precision=UPPER_LIMIT)
```

```python
import jax
import jax.numpy as jnp
from jax import lax
from jax.experimental import pallas as pl
from jax.experimental.pallas import tpu as pltpu
from jax.sharding import PartitionSpec as P

SYSTEM = (0, 0, 0, 1, 2)
F32 = jnp.float32
TILE = (8, 128)


def iotas():
    sub = lax.broadcasted_iota(jnp.int32, TILE, 0)
    lane = lax.broadcasted_iota(jnp.int32, TILE, 1)
    return sub, lane


def roll(x, shift, axis):
    size = x.shape[axis]
    return pltpu.roll(x, shift % size if isinstance(shift, int) else shift, axis)


def primitives(q):
    inv = 1.0 / jnp.where(q[0] == 0.0, 1.0, q[0])
    kinetic = 0.5 * (q[1] * q[1] + q[2] * q[2] + q[3] * q[3]) * inv
    return inv, 0.4 * (q[4] - kinetic)


def flux(q, inv, pressure, k):
    velocity = q[1 + k] * inv
    parts = [q[1 + k], q[1] * velocity, q[2] * velocity, q[3] * velocity, (q[4] + pressure) * velocity]
    parts[1 + k] = parts[1 + k] + pressure
    return parts


def quarter_move(x, a, b):
    return x if a == b else roll(x, 32 * (b - a), 1)


def by_quarter(lane, xs):
    return jnp.where(
        lane < 64, jnp.where(lane < 32, xs[0], xs[1]), jnp.where(lane < 96, xs[2], xs[3])
    )


def edges_kernel(cells, x_ref, lower_ref, upper_ref, edge_ref, last_ref, first_ref, coef_ref):
    sub, lane = iotas()
    left = sub < 4
    packed = []
    for v in range(5):
        total = jnp.zeros(TILE, F32)
        for i in range(cells):
            moved = roll(x_ref[pl.ds((v * cells + i) * 8, 8), :], i, 1)
            total = jnp.where(lane == jnp.where(left, i, (i - 1) % 128), moved, total)
        total = roll(total, 4, 0)
        packed.append(jnp.where(left, roll(total, 1, 1), roll(total, 127, 1)))
        for n in range(2):
            last_ref[pl.ds((v * 2 + n) * 8, 8), :] = x_ref[pl.ds((v * cells + cells - 2 + n) * 8, 8), :]
            first_ref[pl.ds((v * 2 + n) * 8, 8), :] = x_ref[pl.ds((v * cells + n) * 8, 8), :]
    inv, pressure = primitives(packed)
    for v, part in enumerate(flux(packed, inv, pressure, 1)):
        edge_ref[pl.ds(v * 8, 8), :] = part
    coef_ref[...] = jnp.zeros(coef_ref.shape, F32)
    for s in range(3):
        inverse = 1.0 / lower_ref[s, 2:3, :]
        coef_ref[s * 5 : s * 5 + 1, 0:cells] = lower_ref[s, 1:2, :] * inverse
        coef_ref[s * 5 + 1 : s * 5 + 2, 0:cells] = lower_ref[s, 0:1, :] * inverse
        coef_ref[s * 5 + 2 : s * 5 + 3, 0:cells] = inverse
        coef_ref[s * 5 + 3 : s * 5 + 5, 0:cells] = upper_ref[s]


def local_kernel(
    cells, x_ref, dt_ref, before_ref, after_ref, west_ref, east_ref, coef_ref, char_mat, char_ref, out_ref, q_ref, f_ref
):
    sub, lane = iotas()
    third = sub % 4
    west = sub < 4
    for v in range(5):
        q_ref[v, 0:16] = before_ref[pl.ds(v * 16, 16), :]
        q_ref[v, pl.ds(16, cells * 8)] = x_ref[pl.ds(v * cells * 8, cells * 8), :]
        q_ref[v, pl.ds(16 + cells * 8, 16)] = after_ref[pl.ds(v * 16, 16), :]
    beside = [
        jnp.where(west, west_ref[pl.ds(v * 8, 8), :], east_ref[pl.ds(v * 8, 8), :]) for v in range(5)
    ]
    outside = (west & (lane == 0)) | (~west & (lane == 127))
    unit = [jnp.where((lane == n) & (sub >= 0), 1.0, 0.0).astype(F32) for n in range(4)]
    zero = jnp.where((lane < 0) & (sub < 0), 1.0, 0.0).astype(F32)
    rows = SYSTEM + (0, 1, 2)

    def layer(i):
        at = pl.ds(pl.multiple_of((i + 2) * 8, 8), 8)
        return [q_ref[v, at, :] for v in range(5)]

    def line(i):
        q = layer(i)
        inv, pressure = primitives(q)
        return flux(q, inv, pressure, 0), inv, pressure

    def forward(i, carry):
        flux_before, (flux_now, inv, pressure), prior_one, prior_two = carry
        q = layer(i)
        flux_after, inv_after, pressure_after = line(i + 1)
        side = flux(q, inv, pressure, 1)
        over = flux(q, inv, pressure, 2)
        two, one, next_one, next_two = (layer(i + n) for n in (-2, -1, 1, 2))
        scale = -0.5 * dt_ref[pl.ds(pl.multiple_of(i * 8, 8), 8), :]
        right = []
        for v in range(5):
            down, up = roll(side[v], 1, 1), roll(side[v], 127, 1)
            cut = roll(jnp.where(lane == 0, down, up), 4, 0)
            cut = jnp.where(outside, roll(beside[v], lax.rem(128 - i, 128), 1), cut)
            side_diff = jnp.where(lane == 127, cut, up) - jnp.where(lane == 0, cut, down)
            over_diff = jnp.where(third == 3, roll(over[v], 3, 0), roll(over[v], 7, 0)) - jnp.where(
                third == 0, roll(over[v], 5, 0), roll(over[v], 1, 0)
            )
            fourth = (two[v] + next_two[v]) - 4.0 * (one[v] + next_one[v]) + 6.0 * q[v]
            total = (flux_after[v] - flux_before[v]) + side_diff + over_diff + 0.125 * fourth
            right.append(scale * total)
        new = []
        for n, s in enumerate(rows):
            value = -(coef_ref[s * 5, i] * prior_one[n]) - coef_ref[s * 5 + 1, i] * prior_two[n]
            if n < 5:
                char = sum(char_mat[n, v] * right[v] for v in range(5))
                char_ref[pl.ds(pl.multiple_of((n * cells + i) * 8, 8), 8), :] = char
                value = value + coef_ref[s * 5 + 2, i] * char
            f_ref[n, pl.ds(pl.multiple_of(i * 8, 8), 8), :] = value
            new.append(value)
        return flux_now, (flux_after, inv_after, pressure_after), new, prior_one

    start = [zero] * 5
    _, _, last_one, last_two = lax.fori_loop(
        0,
        cells,
        forward,
        (line(-1)[0], line(0), start + [unit[0]] * 3, start + [unit[1]] * 3),
    )

    def backward(step, carry):
        i = cells - 1 - step
        next_one, next_two = carry
        new = []
        for n, s in enumerate(rows):
            value = f_ref[n, pl.ds(pl.multiple_of(i * 8, 8), 8), :]
            new.append(value - coef_ref[s * 5 + 3, i] * next_one[n] - coef_ref[s * 5 + 4, i] * next_two[n])
        return new, next_one

    first_one, first_two = lax.fori_loop(
        0, cells, backward, (start + [unit[2]] * 3, start + [unit[3]] * 3)
    )
    ends = (last_one, last_two, first_one, first_two)
    response = zero
    for s in range(3):
        for k in range(4):
            at = (s * 4 + k) * 4
            moved = ends[k][5 + s] if at == 0 else roll(ends[k][5 + s], at, 1)
            response = jnp.where((lane >= at) & (lane < at + 4), moved, response)
    for quarter in range(4):
        base = quarter * 64
        for k in range(4):
            out_ref[pl.ds(base + k, 8, stride=8), :] = by_quarter(
                lane, [quarter_move(ends[k][u], quarter, u) for u in range(4)]
            )
        out_ref[pl.ds(base + 4, 8, stride=8), :] = by_quarter(
            lane, [quarter_move(ends[k][4], quarter, k) for k in range(4)]
        )
        out_ref[pl.ds(base + 5, 8, stride=8), :] = jnp.broadcast_to(response[0:1, :], TILE)
        for k in (6, 7):
            out_ref[pl.ds(base + k, 8, stride=8), :] = zero


def reduced_kernel(count, in_ref, out_ref, part_ref, coef_ref, four_ref):
    lane = lax.broadcasted_iota(jnp.int32, (count, 128), 1)
    fifth = in_ref[pl.ds(4, count, stride=8), :]
    response = in_ref[pl.ds(5, count, stride=8), :]
    for k in range(4):
        part_ref[k, 0] = in_ref[pl.ds(k, count, stride=8), :]
        part_ref[k, 1] = quarter_move(fifth, k, 0)
        for c in range(4):
            if k < 2 and c >= 2:
                continue
            wide = [
                jnp.broadcast_to(response[:, (s * 4 + k) * 4 + c : (s * 4 + k) * 4 + c + 1], (count, 128))
                for s in range(3)
            ]
            coef_ref[k * 4 + c, 0] = jnp.where(lane < 96, wide[0], wide[1])
            coef_ref[k * 4 + c, 1] = wide[2]
    zero = jnp.zeros((1, 128), F32)

    def take(ref, n, tile, t):
        return ref[n, tile, t : t + 1, :]

    inflow = [(zero, zero), (zero, zero)]
    sums = []
    for t in range(count):
        row = []
        for tile in range(2):
            one, two = inflow[tile]
            for k, value in ((0, one), (1, two)):
                if tile == 0:
                    out_ref[t * 8 + k : t * 8 + k + 1, :] = value
                else:
                    four_ref[k, t : t + 1, :] = value
            made = [
                take(part_ref, k, tile, t)
                + take(coef_ref, k * 4, tile, t) * one
                + take(coef_ref, k * 4 + 1, tile, t) * two
                for k in range(4)
            ]
            inflow[tile] = (made[0], made[1])
            row.append((made[2], made[3]))
        sums.append(row)
    inflow = [(zero, zero), (zero, zero)]
    for t in reversed(range(count)):
        for tile in range(2):
            one, two = inflow[tile]
            for k, value in ((2, one), (3, two)):
                if tile == 0:
                    out_ref[t * 8 + k : t * 8 + k + 1, :] = value
                else:
                    four_ref[k, t : t + 1, :] = value
            inflow[tile] = tuple(
                sums[t][tile][k - 2]
                + take(coef_ref, k * 4 + 2, tile, t) * one
                + take(coef_ref, k * 4 + 3, tile, t) * two
                for k in (2, 3)
            )
    out_ref[pl.ds(4, count, stride=8), :] = by_quarter(
        lane, [quarter_move(four_ref[k], 0, k) for k in range(4)]
    )
    for k in (5, 6, 7):
        out_ref[pl.ds(k, count, stride=8), :] = jnp.zeros((count, 128), F32)


def final_kernel(cells, char_ref, in_ref, coef_ref, cons_mat, out_ref, f_ref):
    _, lane = iotas()
    inflow = []
    for k in range(4):
        parts = [in_ref[pl.ds(q * 64 + k, 8, stride=8), :] for q in range(4)]
        inflow.append(
            [by_quarter(lane, [quarter_move(parts[q], u, q) for q in range(4)]) for u in range(4)]
        )
    parts = [in_ref[pl.ds(q * 64 + 4, 8, stride=8), :] for q in range(4)]
    for k in range(4):
        inflow[k].append(by_quarter(lane, [quarter_move(parts[q], k, q) for q in range(4)]))

    def forward(i, carry):
        prior_one, prior_two = carry
        new = []
        for n, s in enumerate(SYSTEM):
            value = coef_ref[s * 5 + 2, i] * char_ref[pl.ds(pl.multiple_of((n * cells + i) * 8, 8), 8), :]
            value = value - coef_ref[s * 5 + 1, i] * prior_two[n] - coef_ref[s * 5, i] * prior_one[n]
            f_ref[n, pl.ds(pl.multiple_of(i * 8, 8), 8), :] = value
            new.append(value)
        return new, prior_one

    lax.fori_loop(0, cells, forward, (inflow[0], inflow[1]))

    def backward(step, carry):
        i = cells - 1 - step
        next_one, next_two = carry
        new = []
        for n, s in enumerate(SYSTEM):
            value = f_ref[n, pl.ds(pl.multiple_of(i * 8, 8), 8), :]
            new.append(value - coef_ref[s * 5 + 4, i] * next_two[n] - coef_ref[s * 5 + 3, i] * next_one[n])
        for n in range(5):
            out_ref[pl.ds(pl.multiple_of((n * cells + i) * 8, 8), 8), :] = sum(
                cons_mat[n, v] * new[v] for v in range(5)
            )
        return new, next_one

    lax.fori_loop(0, cells, backward, (inflow[2], inflow[3]))


def shaped(*shape):
    return jax.ShapeDtypeStruct(shape, F32)


VMEM = pl.BlockSpec(memory_space=pltpu.VMEM)
SMEM = pl.BlockSpec(memory_space=pltpu.SMEM)


def on_device(state, time_step, to_char, to_cons, lower_bands, upper_bands):
    cells = state.shape[1]
    count = lax.axis_size("sec")
    columns = lax.axis_size("cross")
    flat = state.reshape(5, cells, 4, 2, 128).transpose(0, 1, 3, 2, 4).reshape(5 * cells * 8, 128)
    steps = time_step.reshape(cells, 4, 2, 128).transpose(0, 2, 1, 3).reshape(cells * 8, 128)
    edge, last, first, coef = pl.pallas_call(
        lambda *refs: edges_kernel(cells, *refs),
        out_shape=(shaped(40, 128), shaped(80, 128), shaped(80, 128), shaped(16, 128)),
        in_specs=[VMEM] * 3,
        out_specs=(VMEM,) * 4,
        name="edges",
    )(flat, lower_bands, upper_bands)
    up = [(i, i + 1) for i in range(count - 1)]
    right = [(i, i + 1) for i in range(columns - 1)]
    before = lax.ppermute(last, "sec", up)
    after = lax.ppermute(first, "sec", [(j, i) for i, j in up])
    west = lax.ppermute(edge, "cross", right)
    east = lax.ppermute(edge, "cross", [(j, i) for i, j in right])
    char, ends = pl.pallas_call(
        lambda *refs: local_kernel(cells, *refs),
        out_shape=(shaped(5 * cells * 8, 128), shaped(256, 128)),
        in_specs=[VMEM] * 6 + [SMEM] * 2,
        out_specs=(VMEM, VMEM),
        scratch_shapes=[
            pltpu.VMEM((5, (cells + 4) * 8, 128), F32),
            pltpu.VMEM((8, cells * 8, 128), F32),
        ],
        name="local",
    )(flat, steps, before, after, west, east, coef, to_char)
    ends = lax.all_to_all(ends, "sec", 0, 0, tiled=True)
    inflow = pl.pallas_call(
        lambda *refs: reduced_kernel(count, *refs),
        out_shape=shaped(256, 128),
        in_specs=[VMEM],
        out_specs=VMEM,
        scratch_shapes=[
            pltpu.VMEM((4, 2, count, 128), F32),
            pltpu.VMEM((16, 2, count, 128), F32),
            pltpu.VMEM((4, count, 128), F32),
        ],
        name="reduced",
    )(ends)
    inflow = lax.all_to_all(inflow, "sec", 0, 0, tiled=True)
    result = pl.pallas_call(
        lambda *refs: final_kernel(cells, *refs),
        out_shape=shaped(5 * cells * 8, 128),
        in_specs=[VMEM, VMEM, SMEM, SMEM],
        out_specs=VMEM,
        scratch_shapes=[pltpu.VMEM((5, cells * 8, 128), F32)],
        name="final",
    )(char, inflow, coef, to_cons)
    return result.reshape(5, cells, 2, 4, 128).transpose(0, 1, 3, 2, 4).reshape(state.shape)


def solution(mesh):
    in_specs = (
        P(None, "sec", None, "cross"),
        P("sec", None, "cross"),
        P(),
        P(),
        P(None, None, "sec"),
        P(None, None, "sec"),
    )
    out_specs = P(None, "sec", None, "cross")
    return jax.shard_map(
        on_device, mesh=mesh, in_specs=in_specs, out_specs=out_specs, check_vma=False
    )
```

```python
import jax
import jax.numpy as jnp
from jax import lax
from jax.experimental import pallas as pl
from jax.experimental.pallas import tpu as pltpu
from jax.sharding import PartitionSpec as P

SYSTEM = (0, 0, 0, 1, 2)
F32 = jnp.float32
UNROLL = 8
TILE = (8, 128)


def iotas():
    sub = lax.broadcasted_iota(jnp.int32, TILE, 0)
    lane = lax.broadcasted_iota(jnp.int32, TILE, 1)
    return sub, lane


def roll(x, shift, axis):
    size = x.shape[axis]
    return pltpu.roll(x, shift % size if isinstance(shift, int) else shift, axis)


def primitives(q):
    inv = 1.0 / jnp.where(q[0] == 0.0, 1.0, q[0])
    kinetic = 0.5 * (q[1] * q[1] + q[2] * q[2] + q[3] * q[3]) * inv
    return inv, 0.4 * (q[4] - kinetic)


def flux(q, inv, pressure, k):
    velocity = q[1 + k] * inv
    parts = [q[1 + k], q[1] * velocity, q[2] * velocity, q[3] * velocity, (q[4] + pressure) * velocity]
    parts[1 + k] = parts[1 + k] + pressure
    return parts


def quarter_move(x, a, b):
    return x if a == b else roll(x, 32 * (b - a), 1)


def by_quarter(lane, xs):
    return jnp.where(
        lane < 64, jnp.where(lane < 32, xs[0], xs[1]), jnp.where(lane < 96, xs[2], xs[3])
    )


def packed_edges(cells, layer):
    sub, lane = iotas()
    total = jnp.zeros(TILE, F32)
    for i in range(cells):
        moved = roll(layer(i), i, 1) if i else layer(i)
        total = jnp.where(lane == jnp.where(sub < 4, i, (i - 1) % 128), moved, total)
    return total


def edges_kernel(
    cells, x_hbm, dt_hbm, lower_hbm, upper_hbm, char_hbm, cons_hbm,
    edge_ref, last_ref, first_ref, x_ref, dt_ref, dt_edge_ref, coef_ref, char_mat, cons_mat,
    lower_ref, upper_ref, made_ref, x_sems, sems,
):
    sub, _ = iotas()
    rows = cells * 8
    x_copies = [
        pltpu.make_async_copy(
            x_hbm.at[pl.ds(v * rows, rows)], x_ref.at[v, pl.ds(16, rows)], x_sems.at[v]
        )
        for v in range(5)
    ]
    pairs = (
        (lower_hbm, lower_ref),
        (upper_hbm, upper_ref),
        (dt_hbm, dt_ref),
        (char_hbm, char_mat),
        (cons_hbm, cons_mat),
    )
    copies = [pltpu.make_async_copy(a, b, sems.at[n]) for n, (a, b) in enumerate(pairs)]
    for copy in x_copies + copies:
        copy.start()
    for v in range(5):
        x_ref[v, 0:16] = jnp.zeros((16, 128), F32)
        x_ref[v, pl.ds(16 + rows, 16)] = jnp.zeros((16, 128), F32)
    made_ref[...] = jnp.zeros(made_ref.shape, F32)
    copies[0].wait()
    copies[1].wait()
    for s in range(3):
        inverse = 1.0 / lower_ref[s, 2:3, :]
        made_ref[s * 5 : s * 5 + 1, 0:cells] = lower_ref[s, 1:2, :] * inverse
        made_ref[s * 5 + 1 : s * 5 + 2, 0:cells] = lower_ref[s, 0:1, :] * inverse
        made_ref[s * 5 + 2 : s * 5 + 3, 0:cells] = inverse
        made_ref[s * 5 + 3 : s * 5 + 5, 0:cells] = upper_ref[s]
    made = pltpu.make_async_copy(made_ref, coef_ref, sems.at[5])
    made.start()
    packed = []
    for v in range(5):
        x_copies[v].wait()
        total = packed_edges(cells, lambda i, v=v: x_ref[v, pl.ds(16 + i * 8, 8), :])
        total = roll(total, 4, 0)
        packed.append(jnp.where(sub < 4, roll(total, 1, 1), roll(total, 127, 1)))
        last_ref[pl.ds(v * 16, 16), :] = x_ref[v, pl.ds(rows, 16), :]
        first_ref[pl.ds(v * 16, 16), :] = x_ref[v, 16:32, :]
    inv, pressure = primitives(packed)
    for v, part in enumerate(flux(packed, inv, pressure, 1)):
        edge_ref[pl.ds(v * 8, 8), :] = part
    copies[2].wait()
    dt_edge_ref[...] = packed_edges(cells, lambda i: dt_ref[pl.ds(i * 8, 8), :])
    copies[3].wait()
    copies[4].wait()
    made.wait()


def layer_at(i):
    return pl.ds(i * 8 if isinstance(i, int) else pl.multiple_of(i * 8, 8), 8)


def to_char(char_mat, right):
    return [sum(char_mat[u, v] * right[v] for v in range(5)) for u in range(5)]


def inner_kernel(cells, x_ref, dt_ref, coef_ref, char_mat, char_ref, response_ref, f_ref):
    sub, lane = iotas()
    third = sub % 4

    def layer(i):
        return [x_ref[v, layer_at(i + 2), :] for v in range(5)]

    def line(i):
        q = layer(i)
        inv, pressure = primitives(q)
        return flux(q, inv, pressure, 0), inv, pressure

    def cell(i, carry):
        flux_before, (flux_now, inv, pressure) = carry
        q = layer(i)
        flux_after, inv_after, pressure_after = line(i + 1)
        side = flux(q, inv, pressure, 1)
        over = flux(q, inv, pressure, 2)
        two, one, next_one, next_two = (layer(i + n) for n in (-2, -1, 1, 2))
        scale = -0.5 * dt_ref[layer_at(i), :]
        right = []
        for v in range(5):
            down, up = roll(side[v], 1, 1), roll(side[v], 127, 1)
            cut = roll(jnp.where(lane == 0, down, up), 4, 0)
            cut = jnp.where((lane == 0) == (sub < 4), 0.0, cut)
            side_diff = jnp.where(lane == 127, cut, up) - jnp.where(lane == 0, cut, down)
            over_diff = jnp.where(third == 3, roll(over[v], 3, 0), roll(over[v], 7, 0)) - jnp.where(
                third == 0, roll(over[v], 5, 0), roll(over[v], 1, 0)
            )
            fourth = (two[v] + next_two[v]) - 4.0 * (one[v] + next_one[v]) + 6.0 * q[v]
            total = (flux_after[v] - flux_before[v]) + side_diff + over_diff + 0.125 * fourth
            right.append(scale * total)
        for u, value in enumerate(to_char(char_mat, right)):
            char_ref[u, layer_at(i), :] = value
        return flux_now, (flux_after, inv_after, pressure_after)

    lax.fori_loop(0, cells, cell, (line(-1)[0], line(0)), unroll=UNROLL)

    unit = [jnp.where((lane == n) & (sub >= 0), 1.0, 0.0).astype(F32) for n in range(4)]

    def forward(i, carry):
        one, two = carry
        new = [-(coef_ref[s * 5, i] * one[s]) - coef_ref[s * 5 + 1, i] * two[s] for s in range(3)]
        for s in range(3):
            f_ref[s, layer_at(i), :] = new[s]
        return new, one

    def backward(step, carry):
        i = cells - 1 - step
        one, two = carry
        new = [
            f_ref[s, layer_at(i), :] - coef_ref[s * 5 + 3, i] * one[s] - coef_ref[s * 5 + 4, i] * two[s]
            for s in range(3)
        ]
        return new, one

    last = lax.fori_loop(0, cells, forward, ([unit[0]] * 3, [unit[1]] * 3), unroll=UNROLL)
    first = lax.fori_loop(0, cells, backward, ([unit[2]] * 3, [unit[3]] * 3), unroll=UNROLL)
    ends = last + first
    response = jnp.zeros(TILE, F32)
    for s in range(3):
        for k in range(4):
            at = (s * 4 + k) * 4
            moved = ends[k][s] if at == 0 else roll(ends[k][s], at, 1)
            response = jnp.where((lane >= at) & (lane < at + 4), moved, response)
    response_ref[...] = response


def local_kernel(
    cells, char_ref, response_ref, dt_ref, dt_edge_ref, before_ref, after_ref, west_ref, east_ref, coef_ref, char_mat,
    out_ref, f_ref,
):
    sub, lane = iotas()
    before = [[before_ref[pl.ds(v * 16 + n, 8), :] for v in range(5)] for n in (0, 8)]
    after = [[after_ref[pl.ds(v * 16 + n, 8), :] for v in range(5)] for n in (0, 8)]
    flux_before = flux(before[1], *primitives(before[1]), 0)
    flux_after = flux(after[0], *primitives(after[0]), 0)
    terms = (
        (0, lambda v: 0.125 * (before[0][v] - 4.0 * before[1][v]) - flux_before[v]),
        (1, lambda v: 0.125 * before[1][v]),
        (cells - 2, lambda v: 0.125 * after[0][v]),
        (cells - 1, lambda v: 0.125 * (after[1][v] - 4.0 * after[0][v]) + flux_after[v]),
    )
    added = {}
    for i, term in terms:
        scale = -0.5 * dt_ref[pl.ds(i * 8, 8), :]
        added[i] = to_char(char_mat, [scale * term(v) for v in range(5)])
    scale = -0.5 * dt_edge_ref[...]
    beside = to_char(
        char_mat,
        [
            scale * jnp.where(sub < 4, -west_ref[pl.ds(v * 8, 8), :], east_ref[pl.ds(v * 8, 8), :])
            for v in range(5)
        ],
    )
    outside = (lane == jnp.where(sub < 4, 0, 127)) & (sub >= 0)
    zero = jnp.where((lane < 0) & (sub < 0), 1.0, 0.0).astype(F32)

    def forward(i, carry, more=None):
        one, two = carry
        new = []
        for n, s in enumerate(SYSTEM):
            char = char_ref[n, layer_at(i), :] + jnp.where(
                outside, roll(beside[n], (128 - i) % 128, 1), 0.0
            )
            if more:
                char = char + more[n]
            value = coef_ref[s * 5 + 2, i] * char - coef_ref[s * 5 + 1, i] * two[n] - coef_ref[s * 5, i] * one[n]
            f_ref[n, layer_at(i), :] = value
            new.append(value)
        return new, one

    def backward(step, carry):
        i = cells - 1 - step
        one, two = carry
        new = [
            f_ref[n, layer_at(i), :] - coef_ref[s * 5 + 4, i] * two[n] - coef_ref[s * 5 + 3, i] * one[n]
            for n, s in enumerate(SYSTEM)
        ]
        return new, one

    start = ([zero] * 5, [zero] * 5)
    last = start
    for i in (0, 1):
        last = forward(i, last, added[i])
    last = lax.fori_loop(2, cells - 2, forward, last, unroll=7)
    for i in (cells - 2, cells - 1):
        last = forward(i, last, added[i])
    first = lax.fori_loop(0, cells, backward, start, unroll=UNROLL)
    ends = last + first
    response = jnp.broadcast_to(response_ref[0:1, :], TILE)
    for quarter in range(4):
        base = quarter * 64
        for k in range(4):
            out_ref[pl.ds(base + k, 8, stride=8), :] = by_quarter(
                lane, [quarter_move(ends[k][u], quarter, u) for u in range(4)]
            )
        out_ref[pl.ds(base + 4, 8, stride=8), :] = by_quarter(
            lane, [quarter_move(ends[k][4], quarter, k) for k in range(4)]
        )
        out_ref[pl.ds(base + 5, 8, stride=8), :] = response
        for k in (6, 7):
            out_ref[pl.ds(base + k, 8, stride=8), :] = jnp.zeros(TILE, F32)


def reduced_kernel(count, in_ref, out_ref, part_ref, coef_ref, four_ref):
    lane = lax.broadcasted_iota(jnp.int32, (count, 128), 1)
    fifth = in_ref[pl.ds(4, count, stride=8), :]
    response = in_ref[pl.ds(5, count, stride=8), :]
    for k in range(4):
        part_ref[k, 0] = in_ref[pl.ds(k, count, stride=8), :]
        part_ref[k, 1] = quarter_move(fifth, k, 0)
        for c in range(4):
            if k < 2 and c >= 2:
                continue
            wide = [
                jnp.broadcast_to(response[:, (s * 4 + k) * 4 + c : (s * 4 + k) * 4 + c + 1], (count, 128))
                for s in range(3)
            ]
            coef_ref[k * 4 + c, 0] = jnp.where(lane < 96, wide[0], wide[1])
            coef_ref[k * 4 + c, 1] = wide[2]
    zero = jnp.zeros((1, 128), F32)

    def take(ref, n, tile, t):
        return ref[n, tile, t : t + 1, :]

    inflow = [(zero, zero), (zero, zero)]
    sums = []
    for t in range(count):
        row = []
        for tile in range(2):
            one, two = inflow[tile]
            for k, value in ((0, one), (1, two)):
                if tile == 0:
                    out_ref[t * 8 + k : t * 8 + k + 1, :] = value
                else:
                    four_ref[k, t : t + 1, :] = value
            made = [
                take(part_ref, k, tile, t)
                + take(coef_ref, k * 4, tile, t) * one
                + take(coef_ref, k * 4 + 1, tile, t) * two
                for k in range(4)
            ]
            inflow[tile] = (made[0], made[1])
            row.append((made[2], made[3]))
        sums.append(row)
    inflow = [(zero, zero), (zero, zero)]
    for t in reversed(range(count)):
        for tile in range(2):
            one, two = inflow[tile]
            for k, value in ((2, one), (3, two)):
                if tile == 0:
                    out_ref[t * 8 + k : t * 8 + k + 1, :] = value
                else:
                    four_ref[k, t : t + 1, :] = value
            inflow[tile] = tuple(
                sums[t][tile][k - 2]
                + take(coef_ref, k * 4 + 2, tile, t) * one
                + take(coef_ref, k * 4 + 3, tile, t) * two
                for k in (2, 3)
            )
    out_ref[pl.ds(4, count, stride=8), :] = by_quarter(
        lane, [quarter_move(four_ref[k], 0, k) for k in range(4)]
    )
    for k in (5, 6, 7):
        out_ref[pl.ds(k, count, stride=8), :] = jnp.zeros((count, 128), F32)


def final_kernel(cells, f_ref, in_ref, coef_ref, cons_mat, out_ref, shift_ref):
    _, lane = iotas()
    inflow = []
    for k in range(4):
        parts = [in_ref[pl.ds(q * 64 + k, 8, stride=8), :] for q in range(4)]
        inflow.append(
            [by_quarter(lane, [quarter_move(parts[q], u, q) for q in range(4)]) for u in range(4)]
        )
    parts = [in_ref[pl.ds(q * 64 + 4, 8, stride=8), :] for q in range(4)]
    for k in range(4):
        inflow[k].append(by_quarter(lane, [quarter_move(parts[q], k, q) for q in range(4)]))

    def forward(i, carry):
        one, two = carry
        new = []
        for n, s in enumerate(SYSTEM):
            value = -(coef_ref[s * 5 + 1, i] * two[n]) - coef_ref[s * 5, i] * one[n]
            shift_ref[n, layer_at(i), :] = f_ref[n, layer_at(i), :] + value
            new.append(value)
        return new, one

    lax.fori_loop(0, cells, forward, (inflow[0], inflow[1]), unroll=UNROLL)

    def backward(step, carry):
        i = cells - 1 - step
        one, two = carry
        new = [
            shift_ref[n, layer_at(i), :] - coef_ref[s * 5 + 4, i] * two[n] - coef_ref[s * 5 + 3, i] * one[n]
            for n, s in enumerate(SYSTEM)
        ]
        for n in range(5):
            out_ref[layer_at(n * cells + i), :] = sum(cons_mat[n, v] * new[v] for v in range(5))
        return new, one

    lax.fori_loop(0, cells, backward, (inflow[2], inflow[3]), unroll=UNROLL)


def shaped(*shape):
    return jax.ShapeDtypeStruct(shape, F32)


def kept(*shape):
    return pltpu.VMEM(shape, F32)


def near(x):
    return pltpu.with_memory_space_constraint(x, pltpu.VMEM)


def near_scalars(x):
    return pltpu.with_memory_space_constraint(x, pltpu.SMEM)


VMEM = pl.BlockSpec(memory_space=pltpu.VMEM)
SMEM = pl.BlockSpec(memory_space=pltpu.SMEM)
ANY = pl.BlockSpec(memory_space=pl.ANY)


def on_device(state, time_step, to_char, to_cons, lower_bands, upper_bands):
    cells = state.shape[1]
    count = lax.axis_size("sec")
    columns = lax.axis_size("cross")
    flat = state.reshape(5, cells, 4, 2, 128).transpose(0, 1, 3, 2, 4).reshape(5 * cells * 8, 128)
    steps = time_step.reshape(cells, 4, 2, 128).transpose(0, 2, 1, 3).reshape(cells * 8, 128)
    block = (5, cells * 8, 128)
    edge, last, first, padded, steps, step_edge, coef, char_mat, cons_mat = pl.pallas_call(
        lambda *refs: edges_kernel(cells, *refs),
        out_shape=(
            kept(40, 128),
            kept(80, 128),
            kept(80, 128),
            kept(5, (cells + 4) * 8, 128),
            kept(cells * 8, 128),
            kept(*TILE),
            pltpu.SMEM((16, 128), F32),
            pltpu.SMEM((5, 5), F32),
            pltpu.SMEM((5, 5), F32),
        ),
        in_specs=[ANY] * 6,
        out_specs=(VMEM,) * 6 + (SMEM,) * 3,
        scratch_shapes=[
            pltpu.VMEM(lower_bands.shape, F32),
            pltpu.VMEM(upper_bands.shape, F32),
            pltpu.VMEM((16, 128), F32),
            pltpu.SemaphoreType.DMA((5,)),
            pltpu.SemaphoreType.DMA((6,)),
        ],
        name="edges",
    )(flat, steps, lower_bands, upper_bands, to_char, to_cons)
    coef, char_mat, cons_mat = near_scalars(coef), near_scalars(char_mat), near_scalars(cons_mat)
    up = [(i, i + 1) for i in range(count - 1)]
    right = [(i, i + 1) for i in range(columns - 1)]
    before = near(lax.ppermute(last, "sec", up))
    west = near(lax.ppermute(edge, "cross", right))
    after = near(lax.ppermute(first, "sec", [(j, i) for i, j in up]))
    east = near(lax.ppermute(edge, "cross", [(j, i) for i, j in right]))
    char, response = pl.pallas_call(
        lambda *refs: inner_kernel(cells, *refs),
        out_shape=(kept(*block), kept(*TILE)),
        in_specs=[VMEM] * 2 + [SMEM] * 2,
        out_specs=(VMEM, VMEM),
        scratch_shapes=[pltpu.VMEM((3, cells * 8, 128), F32)],
        name="inner",
    )(near(padded), near(steps), coef, char_mat)
    ends, swept = pl.pallas_call(
        lambda *refs: local_kernel(cells, *refs),
        out_shape=(kept(256, 128), kept(*block)),
        in_specs=[VMEM] * 8 + [SMEM] * 2,
        out_specs=(VMEM, VMEM),
        name="local",
    )(near(char), near(response), near(steps), near(step_edge), before, after, west, east, coef, char_mat)
    ends = lax.all_to_all(ends, "sec", 0, 0, tiled=True)
    inflow = pl.pallas_call(
        lambda *refs: reduced_kernel(count, *refs),
        out_shape=kept(256, 128),
        in_specs=[VMEM],
        out_specs=VMEM,
        scratch_shapes=[
            pltpu.VMEM((4, 2, count, 128), F32),
            pltpu.VMEM((16, 2, count, 128), F32),
            pltpu.VMEM((4, count, 128), F32),
        ],
        name="reduced",
    )(near(ends))
    inflow = lax.all_to_all(inflow, "sec", 0, 0, tiled=True)
    result = pl.pallas_call(
        lambda *refs: final_kernel(cells, *refs),
        out_shape=shaped(5 * cells * 8, 128),
        in_specs=[VMEM, VMEM, SMEM, SMEM],
        out_specs=VMEM,
        scratch_shapes=[pltpu.VMEM(block, F32)],
        name="final",
    )(near(swept), near(inflow), coef, cons_mat)
    return result.reshape(5, cells, 2, 4, 128).transpose(0, 1, 3, 2, 4).reshape(state.shape)


def solution(mesh):
    in_specs = (
        P(None, "sec", None, "cross"),
        P("sec", None, "cross"),
        P(),
        P(),
        P(None, None, "sec"),
        P(None, None, "sec"),
    )
    out_specs = P(None, "sec", None, "cross")
    return jax.shard_map(
        on_device, mesh=mesh, in_specs=in_specs, out_specs=out_specs, check_vma=False
    )
```

```python
import jax
import jax.numpy as jnp
from jax import lax
from jax.experimental import pallas as pl
from jax.experimental.pallas import tpu as pltpu
from jax.sharding import PartitionSpec as P

SYSTEM = (0, 0, 0, 1, 2)
F32 = jnp.float32
CHUNK = 16
UNROLL = 8
TILE = (8, 128)


def iotas():
    sub = lax.broadcasted_iota(jnp.int32, TILE, 0)
    lane = lax.broadcasted_iota(jnp.int32, TILE, 1)
    return sub, lane


def roll(x, shift, axis):
    size = x.shape[axis]
    return pltpu.roll(x, shift % size if isinstance(shift, int) else shift, axis)


def primitives(q):
    inv = 1.0 / jnp.where(q[0] == 0.0, 1.0, q[0])
    kinetic = 0.5 * (q[1] * q[1] + q[2] * q[2] + q[3] * q[3]) * inv
    return inv, 0.4 * (q[4] - kinetic)


def flux(q, inv, pressure, k):
    velocity = q[1 + k] * inv
    parts = [q[1 + k], q[1] * velocity, q[2] * velocity, q[3] * velocity, (q[4] + pressure) * velocity]
    parts[1 + k] = parts[1 + k] + pressure
    return parts


def quarter_move(x, a, b):
    return x if a == b else roll(x, 32 * (b - a), 1)


def by_quarter(lane, xs):
    return jnp.where(
        lane < 64, jnp.where(lane < 32, xs[0], xs[1]), jnp.where(lane < 96, xs[2], xs[3])
    )


def packed_edges(cells, layer):
    sub, lane = iotas()
    total = jnp.zeros(TILE, F32)
    for i in range(cells):
        moved = roll(layer(i), i, 1) if i else layer(i)
        total = jnp.where(lane == jnp.where(sub < 4, i, (i - 1) % 128), moved, total)
    return total


def edges_kernel(
    cells, x_hbm, dt_hbm, lower_hbm, upper_hbm, char_hbm, cons_hbm,
    edge_ref, x_ref, dt_ref, dt_edge_ref, coef_ref, char_mat, cons_mat,
    lower_ref, upper_ref, made_ref, x_sems, sems,
):
    sub, _ = iotas()
    rows = cells * 8
    x_copies = [
        pltpu.make_async_copy(
            x_hbm.at[pl.ds(v * rows, rows)], x_ref.at[v, pl.ds(16, rows)], x_sems.at[v]
        )
        for v in range(5)
    ]
    pairs = (
        (lower_hbm, lower_ref),
        (upper_hbm, upper_ref),
        (dt_hbm, dt_ref),
        (char_hbm, char_mat),
        (cons_hbm, cons_mat),
    )
    copies = [pltpu.make_async_copy(a, b, sems.at[n]) for n, (a, b) in enumerate(pairs)]
    for copy in x_copies + copies:
        copy.start()
    for v in range(5):
        x_ref[v, 0:16] = jnp.zeros((16, 128), F32)
        x_ref[v, pl.ds(16 + rows, 16)] = jnp.zeros((16, 128), F32)
    made_ref[...] = jnp.zeros(made_ref.shape, F32)
    copies[0].wait()
    copies[1].wait()
    for s in range(3):
        inverse = 1.0 / lower_ref[s, 2:3, :]
        made_ref[s * 5 : s * 5 + 1, 0:cells] = lower_ref[s, 1:2, :] * inverse
        made_ref[s * 5 + 1 : s * 5 + 2, 0:cells] = lower_ref[s, 0:1, :] * inverse
        made_ref[s * 5 + 2 : s * 5 + 3, 0:cells] = inverse
        made_ref[s * 5 + 3 : s * 5 + 5, 0:cells] = upper_ref[s]
    made = pltpu.make_async_copy(made_ref, coef_ref, sems.at[5])
    made.start()
    packed = []
    for v in range(5):
        x_copies[v].wait()
        total = packed_edges(cells, lambda i, v=v: x_ref[v, pl.ds(16 + i * 8, 8), :])
        total = roll(total, 4, 0)
        packed.append(jnp.where(sub < 4, roll(total, 1, 1), roll(total, 127, 1)))
    inv, pressure = primitives(packed)
    for v, part in enumerate(flux(packed, inv, pressure, 1)):
        edge_ref[pl.ds(v * 8, 8), :] = part
    copies[2].wait()
    dt_edge_ref[...] = packed_edges(cells, lambda i: dt_ref[pl.ds(i * 8, 8), :])
    copies[3].wait()
    copies[4].wait()
    made.wait()


def layer_at(i):
    return pl.ds(i * 8 if isinstance(i, int) else pl.multiple_of(i * 8, 8), 8)


def to_char(char_mat, right):
    return [sum(char_mat[u, v] * right[v] for v in range(5)) for u in range(5)]


def inner_kernel(cells, x_ref, dt_ref, coef_ref, char_mat, char_ref, give_ref, response_ref, f_ref):
    sub, lane = iotas()
    third = sub % 4

    def layer(i):
        return [x_ref[v, layer_at(i + 2), :] for v in range(5)]

    def line(i):
        q = layer(i)
        inv, pressure = primitives(q)
        return flux(q, inv, pressure, 0), inv, pressure

    def cell(i, carry):
        flux_before, (flux_now, inv, pressure) = carry
        q = layer(i)
        flux_after, inv_after, pressure_after = line(i + 1)
        side = flux(q, inv, pressure, 1)
        over = flux(q, inv, pressure, 2)
        two, one, next_one, next_two = (layer(i + n) for n in (-2, -1, 1, 2))
        scale = -0.5 * dt_ref[layer_at(i), :]
        right = []
        for v in range(5):
            down, up = roll(side[v], 1, 1), roll(side[v], 127, 1)
            cut = roll(jnp.where(lane == 0, down, up), 4, 0)
            cut = jnp.where((lane == 0) == (sub < 4), 0.0, cut)
            side_diff = jnp.where(lane == 127, cut, up) - jnp.where(lane == 0, cut, down)
            over_diff = jnp.where(third == 3, roll(over[v], 3, 0), roll(over[v], 7, 0)) - jnp.where(
                third == 0, roll(over[v], 5, 0), roll(over[v], 1, 0)
            )
            fourth = (two[v] + next_two[v]) - 4.0 * (one[v] + next_one[v]) + 6.0 * q[v]
            total = (flux_after[v] - flux_before[v]) + side_diff + over_diff + 0.125 * fourth
            right.append(scale * total)
        for u, value in enumerate(to_char(char_mat, right)):
            char_ref[u, layer_at(i), :] = value
        return flux_now, (flux_after, inv_after, pressure_after)

    lax.fori_loop(0, cells, cell, (line(-1)[0], line(0)), unroll=UNROLL)

    top, bottom = line(0), line(cells - 1)
    first_two, last_two = (layer(0), layer(1)), (layer(cells - 2), layer(cells - 1))
    gives = (
        [0.125 * (last_two[0][v] - 4.0 * last_two[1][v]) - bottom[0][v] for v in range(5)],
        [0.125 * last_two[1][v] for v in range(5)],
        [0.125 * first_two[0][v] for v in range(5)],
        [0.125 * (first_two[1][v] - 4.0 * first_two[0][v]) + top[0][v] for v in range(5)],
    )
    for m, give in enumerate(gives):
        for u, value in enumerate(to_char(char_mat, give)):
            give_ref[m, u] = value

    unit = [jnp.where((lane == n) & (sub >= 0), 1.0, 0.0).astype(F32) for n in range(8)]

    def forward(i, carry, right=None):
        one, two = carry
        new = []
        for s in range(3):
            value = -(coef_ref[s * 5, i] * one[s]) - coef_ref[s * 5 + 1, i] * two[s]
            if right is not None:
                value = value + coef_ref[s * 5 + 2, i] * right
            f_ref[s, layer_at(i), :] = value
            new.append(value)
        return new, one

    def backward(step, carry):
        i = cells - 1 - step
        one, two = carry
        new = [
            f_ref[s, layer_at(i), :] - coef_ref[s * 5 + 3, i] * one[s] - coef_ref[s * 5 + 4, i] * two[s]
            for s in range(3)
        ]
        return new, one

    last = ([unit[0]] * 3, [unit[1]] * 3)
    for i in (0, 1):
        last = forward(i, last, unit[4 + i])
    last = lax.fori_loop(2, cells - 2, forward, last, unroll=7)
    for i in (0, 1):
        last = forward(cells - 2 + i, last, unit[6 + i])
    first = lax.fori_loop(0, cells, backward, ([unit[2]] * 3, [unit[3]] * 3), unroll=UNROLL)
    ends = last + first
    response = jnp.zeros(TILE, F32)
    for s in range(3):
        for k in range(4):
            at = (s * 4 + k) * 8
            moved = ends[k][s] if at == 0 else roll(ends[k][s], at, 1)
            response = jnp.where((lane >= at) & (lane < at + 8), moved, response)
    response_ref[...] = response


def spread(out_ref, row, lane, groups):
    for quarter in range(4):
        for k, four in enumerate(groups):
            out_ref[pl.ds(quarter * 8 * CHUNK + row + k, 8, stride=CHUNK), :] = by_quarter(
                lane, [quarter_move(four[u], quarter, u) for u in range(4)]
            )


def with_fifth(values):
    return [values[k][:4] for k in range(4)] + [[values[k][4] for k in range(4)]]


def gathered(in_ref, row, lane):
    values = []
    for k in range(5):
        parts = [in_ref[pl.ds(q * 8 * CHUNK + row + k, 8, stride=CHUNK), :] for q in range(4)]
        values.append(
            [by_quarter(lane, [quarter_move(parts[q], u, q) for q in range(4)]) for u in range(4)]
        )
    return [values[k] + [values[4][k]] for k in range(4)]


def local_kernel(
    cells, char_ref, give_ref, response_ref, dt_ref, dt_edge_ref, west_ref, east_ref, coef_ref, char_mat, out_ref, f_ref
):
    sub, lane = iotas()
    scale = -0.5 * dt_edge_ref[...]
    beside = to_char(
        char_mat,
        [
            scale * jnp.where(sub < 4, -west_ref[pl.ds(v * 8, 8), :], east_ref[pl.ds(v * 8, 8), :])
            for v in range(5)
        ],
    )
    outside = (lane == jnp.where(sub < 4, 0, 127)) & (sub >= 0)
    zero = jnp.where((lane < 0) & (sub < 0), 1.0, 0.0).astype(F32)

    def forward(i, carry):
        one, two = carry
        new = []
        for n, s in enumerate(SYSTEM):
            char = char_ref[n, layer_at(i), :] + jnp.where(
                outside, roll(beside[n], (128 - i) % 128, 1), 0.0
            )
            value = coef_ref[s * 5 + 2, i] * char - coef_ref[s * 5 + 1, i] * two[n] - coef_ref[s * 5, i] * one[n]
            f_ref[n, layer_at(i), :] = value
            new.append(value)
        return new, one

    def backward(step, carry):
        i = cells - 1 - step
        one, two = carry
        new = [
            f_ref[n, layer_at(i), :] - coef_ref[s * 5 + 4, i] * two[n] - coef_ref[s * 5 + 3, i] * one[n]
            for n, s in enumerate(SYSTEM)
        ]
        return new, one

    start = ([zero] * 5, [zero] * 5)
    last = lax.fori_loop(0, cells, forward, start, unroll=UNROLL)
    first = lax.fori_loop(0, cells, backward, start, unroll=UNROLL)
    spread(out_ref, 0, lane, with_fifth(last + first))
    spread(out_ref, 6, lane, with_fifth([[give_ref[m, u] for u in range(5)] for m in range(4)]))
    spread(out_ref, 11, lane, [[-0.5 * dt_ref[pl.ds(i * 8, 8), :] for i in (0, 1, cells - 2, cells - 1)]])
    response = jnp.broadcast_to(response_ref[0:1, :], TILE)
    for quarter in range(4):
        base = quarter * 8 * CHUNK
        out_ref[pl.ds(base + 5, 8, stride=CHUNK), :] = response
        for k in range(12, CHUNK):
            out_ref[pl.ds(base + k, 8, stride=CHUNK), :] = jnp.zeros(TILE, F32)


def reduced_kernel(count, in_ref, out_ref, part_ref, coef_ref, four_ref):
    lane = lax.broadcasted_iota(jnp.int32, (count, 128), 1)
    place = lax.broadcasted_iota(jnp.int32, (count, 128), 0)

    def rows(n):
        return in_ref[pl.ds(n, count, stride=CHUNK), :]

    def put(n, value):
        out_ref[pl.ds(n, count, stride=CHUNK), :] = value

    response = rows(5)

    def factor(k, c):
        wide = []
        for s in range(3):
            at = (s * 4 + k) * 8 + c
            wide.append(jnp.broadcast_to(response[:, at : at + 1], (count, 128)))
        return jnp.where(lane < 96, wide[0], wide[1]), wide[2]

    step, fifth = rows(11), rows(10)
    added = []
    for m in range(4):
        scales = by_quarter(lane, [quarter_move(step, m, u) for u in range(4)])
        pair = []
        for give, scale in ((rows(6 + m), scales), (quarter_move(fifth, m, 0), quarter_move(step, m, 0))):
            if m < 2:
                give = jnp.where(place == 0, 0.0, roll(give, 1, 0))
            else:
                give = jnp.where(place == count - 1, 0.0, roll(give, count - 1, 0))
            pair.append(scale * give)
        added.append(pair)
        put(6 + m, pair[0])
    put(10, by_quarter(lane, [quarter_move(added[m][1], 0, m) for m in range(4)]))
    fifth = rows(4)
    for k in range(4):
        values = [rows(k), quarter_move(fifth, k, 0)]
        for m in range(4):
            for tile, part in enumerate(factor(k, 4 + m)):
                values[tile] = values[tile] + part * added[m][tile]
        for tile in range(2):
            part_ref[k, tile] = values[tile]
        for c in range(2 if k < 2 else 4):
            for tile, part in enumerate(factor(k, c)):
                coef_ref[k * 4 + c, tile] = part
    zero = jnp.zeros((1, 128), F32)

    def take(ref, n, tile, t):
        return ref[n, tile, t : t + 1, :]

    inflow = [(zero, zero), (zero, zero)]
    sums = []
    for t in range(count):
        row = []
        for tile in range(2):
            one, two = inflow[tile]
            for k, value in ((0, one), (1, two)):
                if tile == 0:
                    out_ref[t * CHUNK + k : t * CHUNK + k + 1, :] = value
                else:
                    four_ref[k, t : t + 1, :] = value
            made = [
                take(part_ref, k, tile, t)
                + take(coef_ref, k * 4, tile, t) * one
                + take(coef_ref, k * 4 + 1, tile, t) * two
                for k in range(4)
            ]
            inflow[tile] = (made[0], made[1])
            row.append((made[2], made[3]))
        sums.append(row)
    inflow = [(zero, zero), (zero, zero)]
    for t in reversed(range(count)):
        for tile in range(2):
            one, two = inflow[tile]
            for k, value in ((2, one), (3, two)):
                if tile == 0:
                    out_ref[t * CHUNK + k : t * CHUNK + k + 1, :] = value
                else:
                    four_ref[k, t : t + 1, :] = value
            inflow[tile] = tuple(
                sums[t][tile][k - 2]
                + take(coef_ref, k * 4 + 2, tile, t) * one
                + take(coef_ref, k * 4 + 3, tile, t) * two
                for k in (2, 3)
            )
    put(4, by_quarter(lane, [quarter_move(four_ref[k], 0, k) for k in range(4)]))
    for k in (5,) + tuple(range(11, CHUNK)):
        put(k, jnp.zeros((count, 128), F32))


def final_kernel(cells, f_ref, in_ref, coef_ref, cons_mat, out_ref, shift_ref):
    _, lane = iotas()
    inflow = gathered(in_ref, 0, lane)
    added = gathered(in_ref, 6, lane)

    def forward(i, carry, right=None):
        one, two = carry
        new = []
        for n, s in enumerate(SYSTEM):
            value = -(coef_ref[s * 5 + 1, i] * two[n]) - coef_ref[s * 5, i] * one[n]
            if right is not None:
                value = value + coef_ref[s * 5 + 2, i] * right[n]
            shift_ref[n, layer_at(i), :] = f_ref[n, layer_at(i), :] + value
            new.append(value)
        return new, one

    last = (inflow[0], inflow[1])
    for i in (0, 1):
        last = forward(i, last, added[i])
    last = lax.fori_loop(2, cells - 2, forward, last, unroll=7)
    for i in (0, 1):
        last = forward(cells - 2 + i, last, added[2 + i])

    def backward(step, carry):
        i = cells - 1 - step
        one, two = carry
        new = [
            shift_ref[n, layer_at(i), :] - coef_ref[s * 5 + 4, i] * two[n] - coef_ref[s * 5 + 3, i] * one[n]
            for n, s in enumerate(SYSTEM)
        ]
        for n in range(5):
            out_ref[layer_at(n * cells + i), :] = sum(cons_mat[n, v] * new[v] for v in range(5))
        return new, one

    lax.fori_loop(0, cells, backward, (inflow[2], inflow[3]), unroll=UNROLL)


def shaped(*shape):
    return jax.ShapeDtypeStruct(shape, F32)


def kept(*shape):
    return pltpu.VMEM(shape, F32)


def near(x):
    return pltpu.with_memory_space_constraint(x, pltpu.VMEM)


def near_scalars(x):
    return pltpu.with_memory_space_constraint(x, pltpu.SMEM)


VMEM = pl.BlockSpec(memory_space=pltpu.VMEM)
SMEM = pl.BlockSpec(memory_space=pltpu.SMEM)
ANY = pl.BlockSpec(memory_space=pl.ANY)


def on_device(state, time_step, to_char, to_cons, lower_bands, upper_bands):
    cells = state.shape[1]
    count = lax.axis_size("sec")
    columns = lax.axis_size("cross")
    flat = state.reshape(5, cells, 4, 2, 128).transpose(0, 1, 3, 2, 4).reshape(5 * cells * 8, 128)
    steps = time_step.reshape(cells, 4, 2, 128).transpose(0, 2, 1, 3).reshape(cells * 8, 128)
    block = (5, cells * 8, 128)
    edge, padded, steps, step_edge, coef, char_mat, cons_mat = pl.pallas_call(
        lambda *refs: edges_kernel(cells, *refs),
        out_shape=(
            kept(40, 128),
            kept(5, (cells + 4) * 8, 128),
            kept(cells * 8, 128),
            kept(*TILE),
            pltpu.SMEM((16, 128), F32),
            pltpu.SMEM((5, 5), F32),
            pltpu.SMEM((5, 5), F32),
        ),
        in_specs=[ANY] * 6,
        out_specs=(VMEM,) * 4 + (SMEM,) * 3,
        scratch_shapes=[
            pltpu.VMEM(lower_bands.shape, F32),
            pltpu.VMEM(upper_bands.shape, F32),
            pltpu.VMEM((16, 128), F32),
            pltpu.SemaphoreType.DMA((5,)),
            pltpu.SemaphoreType.DMA((6,)),
        ],
        name="edges",
    )(flat, steps, lower_bands, upper_bands, to_char, to_cons)
    coef, char_mat, cons_mat = near_scalars(coef), near_scalars(char_mat), near_scalars(cons_mat)
    right = [(i, i + 1) for i in range(columns - 1)]
    west = near(lax.ppermute(edge, "cross", right))
    east = near(lax.ppermute(edge, "cross", [(j, i) for i, j in right]))
    char, give, response = pl.pallas_call(
        lambda *refs: inner_kernel(cells, *refs),
        out_shape=(kept(*block), kept(4, 5, *TILE), kept(*TILE)),
        in_specs=[VMEM] * 2 + [SMEM] * 2,
        out_specs=(VMEM,) * 3,
        scratch_shapes=[pltpu.VMEM((3, cells * 8, 128), F32)],
        name="inner",
    )(near(padded), near(steps), coef, char_mat)
    ends, swept = pl.pallas_call(
        lambda *refs: local_kernel(cells, *refs),
        out_shape=(kept(count * CHUNK, 128), kept(*block)),
        in_specs=[VMEM] * 7 + [SMEM] * 2,
        out_specs=(VMEM, VMEM),
        name="local",
    )(near(char), near(give), near(response), near(steps), near(step_edge), west, east, coef, char_mat)
    ends = lax.all_to_all(ends, "sec", 0, 0, tiled=True)
    inflow = pl.pallas_call(
        lambda *refs: reduced_kernel(count, *refs),
        out_shape=kept(count * CHUNK, 128),
        in_specs=[VMEM],
        out_specs=VMEM,
        scratch_shapes=[
            pltpu.VMEM((4, 2, count, 128), F32),
            pltpu.VMEM((16, 2, count, 128), F32),
            pltpu.VMEM((4, count, 128), F32),
        ],
        name="reduced",
    )(near(ends))
    inflow = lax.all_to_all(inflow, "sec", 0, 0, tiled=True)
    result = pl.pallas_call(
        lambda *refs: final_kernel(cells, *refs),
        out_shape=shaped(5 * cells * 8, 128),
        in_specs=[VMEM, VMEM, SMEM, SMEM],
        out_specs=VMEM,
        scratch_shapes=[pltpu.VMEM(block, F32)],
        name="final",
    )(near(swept), near(inflow), coef, cons_mat)
    return result.reshape(5, cells, 2, 4, 128).transpose(0, 1, 3, 2, 4).reshape(state.shape)


def solution(mesh):
    in_specs = (
        P(None, "sec", None, "cross"),
        P("sec", None, "cross"),
        P(),
        P(),
        P(None, None, "sec"),
        P(None, None, "sec"),
    )
    out_specs = P(None, "sec", None, "cross")
    return jax.shard_map(
        on_device, mesh=mesh, in_specs=in_specs, out_specs=out_specs, check_vma=False
    )
```

```python
import jax
import jax.numpy as jnp
from jax import lax
from jax.experimental import pallas as pl
from jax.experimental.pallas import tpu as pltpu
from jax.sharding import PartitionSpec as P

SYSTEM = (0, 0, 0, 1, 2)
F32 = jnp.float32
OUT = 12
BACK = 10
UNROLL = 32
TILE = (8, 128)


def iotas():
    sub = lax.broadcasted_iota(jnp.int32, TILE, 0)
    lane = lax.broadcasted_iota(jnp.int32, TILE, 1)
    return sub, lane


def roll(x, shift, axis):
    size = x.shape[axis]
    return pltpu.roll(x, shift % size if isinstance(shift, int) else shift, axis)


def primitives(q):
    inv = 1.0 / jnp.where(q[0] == 0.0, 1.0, q[0])
    kinetic = 0.5 * (q[1] * q[1] + q[2] * q[2] + q[3] * q[3]) * inv
    return inv, 0.4 * (q[4] - kinetic)


def flux(q, inv, pressure, k):
    velocity = q[1 + k] * inv
    parts = [q[1 + k], q[1] * velocity, q[2] * velocity, q[3] * velocity, (q[4] + pressure) * velocity]
    parts[1 + k] = parts[1 + k] + pressure
    return parts


def quarter_move(x, a, b):
    return x if a == b else roll(x, 32 * (b - a), 1)


def by_quarter(lane, xs):
    return jnp.where(
        lane < 64, jnp.where(lane < 32, xs[0], xs[1]), jnp.where(lane < 96, xs[2], xs[3])
    )


def packed_edges(cells, layer):
    sub, lane = iotas()
    total = jnp.zeros(TILE, F32)
    for i in range(cells):
        moved = roll(layer(i), i, 1) if i else layer(i)
        total = jnp.where(lane == jnp.where(sub < 4, i, (i - 1) % 128), moved, total)
    return total


def edges_kernel(
    cells, x_hbm, dt_hbm, lower_hbm, upper_hbm, char_hbm, cons_hbm,
    edge_ref, x_ref, dt_ref, dt_edge_ref, coef_ref, char_mat, cons_mat,
    lower_ref, upper_ref, made_ref, x_sems, sems,
):
    sub, _ = iotas()
    rows = cells * 8
    x_copies = [
        pltpu.make_async_copy(
            x_hbm.at[pl.ds(v * rows, rows)], x_ref.at[v, pl.ds(16, rows)], x_sems.at[v]
        )
        for v in range(5)
    ]
    pairs = (
        (lower_hbm, lower_ref),
        (upper_hbm, upper_ref),
        (dt_hbm, dt_ref),
        (char_hbm, char_mat),
        (cons_hbm, cons_mat),
    )
    copies = [pltpu.make_async_copy(a, b, sems.at[n]) for n, (a, b) in enumerate(pairs)]
    for copy in x_copies + copies:
        copy.start()
    for v in range(5):
        x_ref[v, 0:16] = jnp.zeros((16, 128), F32)
        x_ref[v, pl.ds(16 + rows, 16)] = jnp.zeros((16, 128), F32)
    made_ref[...] = jnp.zeros(made_ref.shape, F32)
    copies[0].wait()
    copies[1].wait()
    for s in range(3):
        inverse = 1.0 / lower_ref[s, 2:3, :]
        made_ref[s * 5 : s * 5 + 1, 0:cells] = lower_ref[s, 1:2, :] * inverse
        made_ref[s * 5 + 1 : s * 5 + 2, 0:cells] = lower_ref[s, 0:1, :] * inverse
        made_ref[s * 5 + 2 : s * 5 + 3, 0:cells] = inverse
        made_ref[s * 5 + 3 : s * 5 + 5, 0:cells] = upper_ref[s]
    made = pltpu.make_async_copy(made_ref, coef_ref, sems.at[5])
    made.start()
    packed = []
    for v in range(5):
        x_copies[v].wait()
        total = packed_edges(cells, lambda i, v=v: x_ref[v, pl.ds(16 + i * 8, 8), :])
        total = roll(total, 4, 0)
        packed.append(jnp.where(sub < 4, roll(total, 1, 1), roll(total, 127, 1)))
    inv, pressure = primitives(packed)
    for v, part in enumerate(flux(packed, inv, pressure, 1)):
        edge_ref[pl.ds(v * 8, 8), :] = part
    copies[2].wait()
    dt_edge_ref[...] = packed_edges(cells, lambda i: dt_ref[pl.ds(i * 8, 8), :])
    copies[3].wait()
    copies[4].wait()
    made.wait()


def layer_at(i):
    return pl.ds(i * 8 if isinstance(i, int) else pl.multiple_of(i * 8, 8), 8)


def to_char(char_mat, right):
    return [sum(char_mat[u, v] * right[v] for v in range(5)) for u in range(5)]


def inner_kernel(cells, x_ref, dt_ref, coef_ref, char_mat, char_ref, give_ref, response_ref, f_ref):
    sub, lane = iotas()
    third = sub % 4

    def layer(i):
        return [x_ref[v, layer_at(i + 2), :] for v in range(5)]

    def line(i):
        q = layer(i)
        inv, pressure = primitives(q)
        return flux(q, inv, pressure, 0), inv, pressure

    def cell(i, carry):
        flux_before, (flux_now, inv, pressure) = carry
        q = layer(i)
        flux_after, inv_after, pressure_after = line(i + 1)
        side = flux(q, inv, pressure, 1)
        over = flux(q, inv, pressure, 2)
        two, one, next_one, next_two = (layer(i + n) for n in (-2, -1, 1, 2))
        scale = -0.5 * dt_ref[layer_at(i), :]
        right = []
        for v in range(5):
            down, up = roll(side[v], 1, 1), roll(side[v], 127, 1)
            cut = roll(jnp.where(lane == 0, down, up), 4, 0)
            cut = jnp.where((lane == 0) == (sub < 4), 0.0, cut)
            side_diff = jnp.where(lane == 127, cut, up) - jnp.where(lane == 0, cut, down)
            over_diff = jnp.where(third == 3, roll(over[v], 3, 0), roll(over[v], 7, 0)) - jnp.where(
                third == 0, roll(over[v], 5, 0), roll(over[v], 1, 0)
            )
            fourth = (two[v] + next_two[v]) - 4.0 * (one[v] + next_one[v]) + 6.0 * q[v]
            total = (flux_after[v] - flux_before[v]) + side_diff + over_diff + 0.125 * fourth
            right.append(scale * total)
        for u, value in enumerate(to_char(char_mat, right)):
            char_ref[u, layer_at(i), :] = value
        return flux_now, (flux_after, inv_after, pressure_after)

    lax.fori_loop(0, cells, cell, (line(-1)[0], line(0)), unroll=UNROLL)

    top, bottom = line(0), line(cells - 1)
    first_two, last_two = (layer(0), layer(1)), (layer(cells - 2), layer(cells - 1))
    gives = (
        [0.125 * (last_two[0][v] - 4.0 * last_two[1][v]) - bottom[0][v] for v in range(5)],
        [0.125 * last_two[1][v] for v in range(5)],
        [0.125 * first_two[0][v] for v in range(5)],
        [0.125 * (first_two[1][v] - 4.0 * first_two[0][v]) + top[0][v] for v in range(5)],
    )
    for m, give in enumerate(gives):
        for u, value in enumerate(to_char(char_mat, give)):
            give_ref[m, u] = value

    unit = [jnp.where((lane == n) & (sub >= 0), 1.0, 0.0).astype(F32) for n in range(8)]

    def forward(i, carry, right=None):
        one, two = carry
        new = []
        for s in range(3):
            value = -(coef_ref[s * 5, i] * one[s]) - coef_ref[s * 5 + 1, i] * two[s]
            if right is not None:
                value = value + coef_ref[s * 5 + 2, i] * right
            f_ref[s, layer_at(i), :] = value
            new.append(value)
        return new, one

    def backward(step, carry):
        i = cells - 1 - step
        one, two = carry
        new = [
            f_ref[s, layer_at(i), :] - coef_ref[s * 5 + 3, i] * one[s] - coef_ref[s * 5 + 4, i] * two[s]
            for s in range(3)
        ]
        return new, one

    last = ([unit[0]] * 3, [unit[1]] * 3)
    for i in (0, 1):
        last = forward(i, last, unit[4 + i])
    last = lax.fori_loop(2, cells - 2, forward, last, unroll=7)
    for i in (0, 1):
        last = forward(cells - 2 + i, last, unit[6 + i])
    first = lax.fori_loop(0, cells, backward, ([unit[2]] * 3, [unit[3]] * 3), unroll=UNROLL)
    ends = last + first
    response = jnp.zeros(TILE, F32)
    for s in range(3):
        for k in range(4):
            at = (s * 4 + k) * 8
            moved = ends[k][s] if at == 0 else roll(ends[k][s], at, 1)
            response = jnp.where((lane >= at) & (lane < at + 8), moved, response)
    response_ref[...] = response


def spread(out_ref, row, lane, groups):
    for quarter in range(4):
        for k, four in enumerate(groups):
            out_ref[pl.ds(quarter * 8 * OUT + row + k, 8, stride=OUT), :] = by_quarter(
                lane, [quarter_move(four[u], quarter, u) for u in range(4)]
            )


def with_fifth(values):
    return [values[k][:4] for k in range(4)] + [[values[k][4] for k in range(4)]]


def gathered(in_ref, row, lane):
    values = []
    for k in range(5):
        parts = [in_ref[pl.ds(q * 8 * BACK + row + k, 8, stride=BACK), :] for q in range(4)]
        values.append(
            [by_quarter(lane, [quarter_move(parts[q], u, q) for q in range(4)]) for u in range(4)]
        )
    return [values[k] + [values[4][k]] for k in range(4)]


def local_kernel(
    cells, char_ref, give_ref, response_ref, dt_ref, dt_edge_ref, west_ref, east_ref, coef_ref, char_mat, out_ref, f_ref
):
    sub, lane = iotas()
    scale = -0.5 * dt_edge_ref[...]
    beside = to_char(
        char_mat,
        [
            scale * jnp.where(sub < 4, -west_ref[pl.ds(v * 8, 8), :], east_ref[pl.ds(v * 8, 8), :])
            for v in range(5)
        ],
    )
    outside = (lane == jnp.where(sub < 4, 0, 127)) & (sub >= 0)
    zero = jnp.where((lane < 0) & (sub < 0), 1.0, 0.0).astype(F32)

    def forward(i, carry):
        one, two = carry
        new = []
        for n, s in enumerate(SYSTEM):
            char = char_ref[n, layer_at(i), :] + jnp.where(
                outside, roll(beside[n], (128 - i) % 128, 1), 0.0
            )
            value = coef_ref[s * 5 + 2, i] * char - coef_ref[s * 5 + 1, i] * two[n] - coef_ref[s * 5, i] * one[n]
            f_ref[n, layer_at(i), :] = value
            new.append(value)
        return new, one

    def backward(step, carry):
        i = cells - 1 - step
        one, two = carry
        new = [
            f_ref[n, layer_at(i), :] - coef_ref[s * 5 + 4, i] * two[n] - coef_ref[s * 5 + 3, i] * one[n]
            for n, s in enumerate(SYSTEM)
        ]
        return new, one

    start = ([zero] * 5, [zero] * 5)
    last = lax.fori_loop(0, cells, forward, start, unroll=UNROLL)
    first = lax.fori_loop(0, cells, backward, start, unroll=UNROLL)
    spread(out_ref, 0, lane, with_fifth(last + first))
    spread(out_ref, 6, lane, with_fifth([[give_ref[m, u] for u in range(5)] for m in range(4)]))
    spread(out_ref, 11, lane, [[-0.5 * dt_ref[pl.ds(i * 8, 8), :] for i in (0, 1, cells - 2, cells - 1)]])
    response = jnp.broadcast_to(response_ref[0:1, :], TILE)
    for quarter in range(4):
        out_ref[pl.ds(quarter * 8 * OUT + 5, 8, stride=OUT), :] = response


def reduced_kernel(count, in_ref, out_ref, part_ref, coef_ref, four_ref):
    lane = lax.broadcasted_iota(jnp.int32, (count, 128), 1)
    place = lax.broadcasted_iota(jnp.int32, (count, 128), 0)

    def rows(n):
        return in_ref[pl.ds(n, count, stride=OUT), :]

    def put(n, value):
        out_ref[pl.ds(n, count, stride=BACK), :] = value

    response = rows(5)

    def factor(k, c):
        wide = []
        for s in range(3):
            at = (s * 4 + k) * 8 + c
            wide.append(jnp.broadcast_to(response[:, at : at + 1], (count, 128)))
        return jnp.where(lane < 96, wide[0], wide[1]), wide[2]

    step, fifth = rows(11), rows(10)
    added = []
    for m in range(4):
        scales = by_quarter(lane, [quarter_move(step, m, u) for u in range(4)])
        pair = []
        for give, scale in ((rows(6 + m), scales), (quarter_move(fifth, m, 0), quarter_move(step, m, 0))):
            if m < 2:
                give = jnp.where(place == 0, 0.0, roll(give, 1, 0))
            else:
                give = jnp.where(place == count - 1, 0.0, roll(give, count - 1, 0))
            pair.append(scale * give)
        added.append(pair)
        put(5 + m, pair[0])
    put(9, by_quarter(lane, [quarter_move(added[m][1], 0, m) for m in range(4)]))
    fifth = rows(4)
    for k in range(4):
        values = [rows(k), quarter_move(fifth, k, 0)]
        for m in range(4):
            for tile, part in enumerate(factor(k, 4 + m)):
                values[tile] = values[tile] + part * added[m][tile]
        for tile in range(2):
            part_ref[k, tile] = values[tile]
        for c in range(2 if k < 2 else 4):
            for tile, part in enumerate(factor(k, c)):
                coef_ref[k * 4 + c, tile] = part
    zero = jnp.zeros((1, 128), F32)

    def take(ref, n, tile, t):
        return ref[n, tile, t : t + 1, :]

    inflow = [(zero, zero), (zero, zero)]
    sums = []
    for t in range(count):
        row = []
        for tile in range(2):
            one, two = inflow[tile]
            for k, value in ((0, one), (1, two)):
                if tile == 0:
                    out_ref[t * BACK + k : t * BACK + k + 1, :] = value
                else:
                    four_ref[k, t : t + 1, :] = value
            made = [
                take(part_ref, k, tile, t)
                + take(coef_ref, k * 4, tile, t) * one
                + take(coef_ref, k * 4 + 1, tile, t) * two
                for k in range(4)
            ]
            inflow[tile] = (made[0], made[1])
            row.append((made[2], made[3]))
        sums.append(row)
    inflow = [(zero, zero), (zero, zero)]
    for t in reversed(range(count)):
        for tile in range(2):
            one, two = inflow[tile]
            for k, value in ((2, one), (3, two)):
                if tile == 0:
                    out_ref[t * BACK + k : t * BACK + k + 1, :] = value
                else:
                    four_ref[k, t : t + 1, :] = value
            inflow[tile] = tuple(
                sums[t][tile][k - 2]
                + take(coef_ref, k * 4 + 2, tile, t) * one
                + take(coef_ref, k * 4 + 3, tile, t) * two
                for k in (2, 3)
            )
    put(4, by_quarter(lane, [quarter_move(four_ref[k], 0, k) for k in range(4)]))


def final_kernel(cells, f_ref, in_ref, coef_ref, cons_mat, out_ref, shift_ref):
    _, lane = iotas()
    inflow = gathered(in_ref, 0, lane)
    added = gathered(in_ref, 5, lane)

    def forward(i, carry, right=None):
        one, two = carry
        new = []
        for n, s in enumerate(SYSTEM):
            value = -(coef_ref[s * 5 + 1, i] * two[n]) - coef_ref[s * 5, i] * one[n]
            if right is not None:
                value = value + coef_ref[s * 5 + 2, i] * right[n]
            shift_ref[n, layer_at(i), :] = f_ref[n, layer_at(i), :] + value
            new.append(value)
        return new, one

    last = (inflow[0], inflow[1])
    for i in (0, 1):
        last = forward(i, last, added[i])
    last = lax.fori_loop(2, cells - 2, forward, last, unroll=7)
    for i in (0, 1):
        last = forward(cells - 2 + i, last, added[2 + i])

    def backward(step, carry):
        i = cells - 1 - step
        one, two = carry
        new = [
            shift_ref[n, layer_at(i), :] - coef_ref[s * 5 + 4, i] * two[n] - coef_ref[s * 5 + 3, i] * one[n]
            for n, s in enumerate(SYSTEM)
        ]
        for n in range(5):
            out_ref[layer_at(n * cells + i), :] = sum(cons_mat[n, v] * new[v] for v in range(5))
        return new, one

    lax.fori_loop(0, cells, backward, (inflow[2], inflow[3]), unroll=UNROLL)


def shaped(*shape):
    return jax.ShapeDtypeStruct(shape, F32)


def kept(*shape):
    return pltpu.VMEM(shape, F32)


def near(x):
    return pltpu.with_memory_space_constraint(x, pltpu.VMEM)


def exchanged(x, count):
    chunks = x.reshape(count, 1, x.size // count)
    return lax.all_to_all(chunks, "sec", 0, 0, tiled=True).reshape(x.shape)


def near_scalars(x):
    return pltpu.with_memory_space_constraint(x, pltpu.SMEM)


VMEM = pl.BlockSpec(memory_space=pltpu.VMEM)
SMEM = pl.BlockSpec(memory_space=pltpu.SMEM)
ANY = pl.BlockSpec(memory_space=pl.ANY)


def on_device(state, time_step, to_char, to_cons, lower_bands, upper_bands):
    cells = state.shape[1]
    count = lax.axis_size("sec")
    columns = lax.axis_size("cross")
    flat = state.reshape(5, cells, 4, 2, 128).transpose(0, 1, 3, 2, 4).reshape(5 * cells * 8, 128)
    steps = time_step.reshape(cells, 4, 2, 128).transpose(0, 2, 1, 3).reshape(cells * 8, 128)
    block = (5, cells * 8, 128)
    edge, padded, steps, step_edge, coef, char_mat, cons_mat = pl.pallas_call(
        lambda *refs: edges_kernel(cells, *refs),
        out_shape=(
            kept(40, 128),
            kept(5, (cells + 4) * 8, 128),
            kept(cells * 8, 128),
            kept(*TILE),
            pltpu.SMEM((16, 128), F32),
            pltpu.SMEM((5, 5), F32),
            pltpu.SMEM((5, 5), F32),
        ),
        in_specs=[ANY] * 6,
        out_specs=(VMEM,) * 4 + (SMEM,) * 3,
        scratch_shapes=[
            pltpu.VMEM(lower_bands.shape, F32),
            pltpu.VMEM(upper_bands.shape, F32),
            pltpu.VMEM((16, 128), F32),
            pltpu.SemaphoreType.DMA((5,)),
            pltpu.SemaphoreType.DMA((6,)),
        ],
        name="edges",
    )(flat, steps, lower_bands, upper_bands, to_char, to_cons)
    coef, char_mat, cons_mat = near_scalars(coef), near_scalars(char_mat), near_scalars(cons_mat)
    right = [(i, i + 1) for i in range(columns - 1)]
    west = near(lax.ppermute(edge, "cross", right))
    east = near(lax.ppermute(edge, "cross", [(j, i) for i, j in right]))
    char, give, response = pl.pallas_call(
        lambda *refs: inner_kernel(cells, *refs),
        out_shape=(kept(*block), kept(4, 5, *TILE), kept(*TILE)),
        in_specs=[VMEM] * 2 + [SMEM] * 2,
        out_specs=(VMEM,) * 3,
        scratch_shapes=[pltpu.VMEM((3, cells * 8, 128), F32)],
        name="inner",
    )(near(padded), near(steps), coef, char_mat)
    ends, swept = pl.pallas_call(
        lambda *refs: local_kernel(cells, *refs),
        out_shape=(kept(count * OUT, 128), kept(*block)),
        in_specs=[VMEM] * 7 + [SMEM] * 2,
        out_specs=(VMEM, VMEM),
        name="local",
    )(near(char), near(give), near(response), near(steps), near(step_edge), west, east, coef, char_mat)
    ends = exchanged(ends, count)
    inflow = pl.pallas_call(
        lambda *refs: reduced_kernel(count, *refs),
        out_shape=kept(count * BACK, 128),
        in_specs=[VMEM],
        out_specs=VMEM,
        scratch_shapes=[
            pltpu.VMEM((4, 2, count, 128), F32),
            pltpu.VMEM((16, 2, count, 128), F32),
            pltpu.VMEM((4, count, 128), F32),
        ],
        name="reduced",
    )(near(ends))
    inflow = exchanged(inflow, count)
    result = pl.pallas_call(
        lambda *refs: final_kernel(cells, *refs),
        out_shape=shaped(5 * cells * 8, 128),
        in_specs=[VMEM, VMEM, SMEM, SMEM],
        out_specs=VMEM,
        scratch_shapes=[pltpu.VMEM(block, F32)],
        name="final",
    )(near(swept), near(inflow), coef, cons_mat)
    return result.reshape(5, cells, 2, 4, 128).transpose(0, 1, 3, 2, 4).reshape(state.shape)


def solution(mesh):
    in_specs = (
        P(None, "sec", None, "cross"),
        P("sec", None, "cross"),
        P(),
        P(),
        P(None, None, "sec"),
        P(None, None, "sec"),
    )
    out_specs = P(None, "sec", None, "cross")
    return jax.shard_map(
        on_device, mesh=mesh, in_specs=in_specs, out_specs=out_specs, check_vma=False
    )
```

```python
import jax
import jax.numpy as jnp
from jax import lax
from jax.experimental import pallas as pl
from jax.experimental.pallas import tpu as pltpu
from jax.sharding import PartitionSpec as P

SYSTEM = (0, 0, 0, 1, 2)
F32 = jnp.float32
OUT = 12
BACK = 12
UNROLL = 32
TILE = (8, 128)


def iotas():
    sub = lax.broadcasted_iota(jnp.int32, TILE, 0)
    lane = lax.broadcasted_iota(jnp.int32, TILE, 1)
    return sub, lane


def roll(x, shift, axis):
    size = x.shape[axis]
    return pltpu.roll(x, shift % size if isinstance(shift, int) else shift, axis)


def primitives(q):
    inv = 1.0 / jnp.where(q[0] == 0.0, 1.0, q[0])
    kinetic = 0.5 * (q[1] * q[1] + q[2] * q[2] + q[3] * q[3]) * inv
    return inv, 0.4 * (q[4] - kinetic)


def flux(q, inv, pressure, k):
    velocity = q[1 + k] * inv
    parts = [q[1 + k], q[1] * velocity, q[2] * velocity, q[3] * velocity, (q[4] + pressure) * velocity]
    parts[1 + k] = parts[1 + k] + pressure
    return parts


def quarter_move(x, a, b):
    return x if a == b else roll(x, 32 * (b - a), 1)


def by_quarter(lane, xs):
    return jnp.where(
        lane < 64, jnp.where(lane < 32, xs[0], xs[1]), jnp.where(lane < 96, xs[2], xs[3])
    )


def packed_edges(cells, layer):
    sub, lane = iotas()
    total = jnp.zeros(TILE, F32)
    for i in range(cells):
        moved = roll(layer(i), i, 1) if i else layer(i)
        total = jnp.where(lane == jnp.where(sub < 4, i, (i - 1) % 128), moved, total)
    return total


def edges_kernel(cells, x_ref, dt_ref, edge_ref, dt_edge_ref):
    sub, _ = iotas()
    packed = []
    for v in range(5):
        total = packed_edges(cells, lambda i, v=v: x_ref[v, pl.ds(16 + i * 8, 8), :])
        total = roll(total, 4, 0)
        packed.append(jnp.where(sub < 4, roll(total, 1, 1), roll(total, 127, 1)))
    inv, pressure = primitives(packed)
    for v, part in enumerate(flux(packed, inv, pressure, 1)):
        edge_ref[pl.ds(v * 8, 8), :] = part
    dt_edge_ref[...] = packed_edges(cells, lambda i: dt_ref[pl.ds(i * 8, 8), :])


def layer_at(i):
    return pl.ds(i * 8 if isinstance(i, int) else pl.multiple_of(i * 8, 8), 8)


def to_char(char_mat, right):
    return [sum(char_mat[u, v] * right[v] for v in range(5)) for u in range(5)]


def spread(out_ref, row, lane, groups):
    for quarter in range(4):
        for k, four in enumerate(groups):
            out_ref[pl.ds(quarter * 8 * OUT + row + k, 8, stride=OUT), :] = by_quarter(
                lane, [quarter_move(four[u], quarter, u) for u in range(4)]
            )


def with_fifth(values):
    return [values[k][:4] for k in range(4)] + [[values[k][4] for k in range(4)]]


def gathered(in_ref, row, lane):
    values = []
    for k in range(5):
        parts = [in_ref[pl.ds(q * 8 * BACK + row + k, 8, stride=BACK), :] for q in range(4)]
        values.append(
            [by_quarter(lane, [quarter_move(parts[q], u, q) for q in range(4)]) for u in range(4)]
        )
    return [values[k] + [values[4][k]] for k in range(4)]


def outer(sub, lane):
    return (lane == jnp.where(sub < 4, 0, 127)) & (sub >= 0)


def swept_back(cells, f_ref, coef_ref):
    def backward(step, carry):
        i = cells - 1 - step
        one, two = carry
        new = [
            f_ref[n, layer_at(i), :] - coef_ref[s * 5 + 4, i] * two[n] - coef_ref[s * 5 + 3, i] * one[n]
            for n, s in enumerate(SYSTEM)
        ]
        return new, one

    return backward


def own_kernel(
    cells, x_hbm, dt_hbm, lower_hbm, upper_hbm, char_hbm, cons_hbm,
    out_ref, f_ref, x_ref, dt_ref, coef_ref, char_mat, cons_mat,
    char_ref, answer_ref, lower_ref, upper_ref, made_ref, x_sems, sems,
):
    sub, lane = iotas()
    rows = cells * 8
    x_copies = [
        pltpu.make_async_copy(
            x_hbm.at[pl.ds(v * rows, rows)], x_ref.at[v, pl.ds(16, rows)], x_sems.at[v]
        )
        for v in range(5)
    ]
    pairs = (
        (lower_hbm, lower_ref),
        (upper_hbm, upper_ref),
        (dt_hbm, dt_ref),
        (char_hbm, char_mat),
        (cons_hbm, cons_mat),
    )
    copies = [pltpu.make_async_copy(a, b, sems.at[n]) for n, (a, b) in enumerate(pairs)]
    for copy in copies[:2] + x_copies + copies[2:]:
        copy.start()
    for v in range(5):
        x_ref[v, 0:16] = jnp.zeros((16, 128), F32)
        x_ref[v, pl.ds(16 + rows, 16)] = jnp.zeros((16, 128), F32)
    made_ref[...] = jnp.zeros(made_ref.shape, F32)
    copies[0].wait()
    copies[1].wait()
    for s in range(3):
        inverse = 1.0 / lower_ref[s, 2:3, :]
        made_ref[s * 5 : s * 5 + 1, 0:cells] = lower_ref[s, 1:2, :] * inverse
        made_ref[s * 5 + 1 : s * 5 + 2, 0:cells] = lower_ref[s, 0:1, :] * inverse
        made_ref[s * 5 + 2 : s * 5 + 3, 0:cells] = inverse
        made_ref[s * 5 + 3 : s * 5 + 5, 0:cells] = upper_ref[s]
    made = pltpu.make_async_copy(made_ref, coef_ref, sems.at[5])
    made.start()
    for copy in x_copies + copies[2:] + [made]:
        copy.wait()

    third = sub % 4

    def layer(i):
        return [x_ref[v, layer_at(i + 2), :] for v in range(5)]

    def line(i):
        q = layer(i)
        inv, pressure = primitives(q)
        return flux(q, inv, pressure, 0), inv, pressure

    def cell(i, carry):
        flux_before, (flux_now, inv, pressure) = carry
        q = layer(i)
        flux_after, inv_after, pressure_after = line(i + 1)
        side = flux(q, inv, pressure, 1)
        over = flux(q, inv, pressure, 2)
        two, one, next_one, next_two = (layer(i + n) for n in (-2, -1, 1, 2))
        scale = -0.5 * dt_ref[layer_at(i), :]
        right = []
        for v in range(5):
            down, up = roll(side[v], 1, 1), roll(side[v], 127, 1)
            cut = roll(jnp.where(lane == 0, down, up), 4, 0)
            cut = jnp.where((lane == 0) == (sub < 4), 0.0, cut)
            side_diff = jnp.where(lane == 127, cut, up) - jnp.where(lane == 0, cut, down)
            over_diff = jnp.where(third == 3, roll(over[v], 3, 0), roll(over[v], 7, 0)) - jnp.where(
                third == 0, roll(over[v], 5, 0), roll(over[v], 1, 0)
            )
            fourth = (two[v] + next_two[v]) - 4.0 * (one[v] + next_one[v]) + 6.0 * q[v]
            total = (flux_after[v] - flux_before[v]) + side_diff + over_diff + 0.125 * fourth
            right.append(scale * total)
        for u, value in enumerate(to_char(char_mat, right)):
            char_ref[u, layer_at(i), :] = value
        return flux_now, (flux_after, inv_after, pressure_after)

    lax.fori_loop(0, cells, cell, (line(-1)[0], line(0)), unroll=UNROLL)
    top, bottom = line(0), line(cells - 1)
    first_two, last_two = (layer(0), layer(1)), (layer(cells - 2), layer(cells - 1))
    gives = (
        [0.125 * (last_two[0][v] - 4.0 * last_two[1][v]) - bottom[0][v] for v in range(5)],
        [0.125 * last_two[1][v] for v in range(5)],
        [0.125 * first_two[0][v] for v in range(5)],
        [0.125 * (first_two[1][v] - 4.0 * first_two[0][v]) + top[0][v] for v in range(5)],
    )
    gives = [to_char(char_mat, give) for give in gives]

    unit = [jnp.where((lane == n) & (sub >= 0), 1.0, 0.0).astype(F32) for n in range(8)]

    def answer(i, carry, right=None):
        one, two = carry
        new = []
        for s in range(3):
            value = -(coef_ref[s * 5, i] * one[s]) - coef_ref[s * 5 + 1, i] * two[s]
            if right is not None:
                value = value + coef_ref[s * 5 + 2, i] * right
            answer_ref[s, layer_at(i), :] = value
            new.append(value)
        return new, one

    def answer_back(step, carry):
        i = cells - 1 - step
        one, two = carry
        new = [
            answer_ref[s, layer_at(i), :] - coef_ref[s * 5 + 3, i] * one[s] - coef_ref[s * 5 + 4, i] * two[s]
            for s in range(3)
        ]
        return new, one

    last = ([unit[0]] * 3, [unit[1]] * 3)
    for i in (0, 1):
        last = answer(i, last, unit[4 + i])
    last = lax.fori_loop(2, cells - 2, answer, last, unroll=7)
    for i in (0, 1):
        last = answer(cells - 2 + i, last, unit[6 + i])
    first = lax.fori_loop(0, cells, answer_back, ([unit[2]] * 3, [unit[3]] * 3), unroll=UNROLL)
    ends = last + first
    response = jnp.zeros(TILE, F32)
    for s in range(3):
        for k in range(4):
            at = (s * 4 + k) * 8
            moved = ends[k][s] if at == 0 else roll(ends[k][s], at, 1)
            response = jnp.where((lane >= at) & (lane < at + 8), moved, response)
    response = jnp.broadcast_to(response[0:1, :], TILE)

    zero = jnp.where((lane < 0) & (sub < 0), 1.0, 0.0).astype(F32)

    def forward(i, carry):
        one, two = carry
        new = []
        for n, s in enumerate(SYSTEM):
            value = coef_ref[s * 5 + 2, i] * char_ref[n, layer_at(i), :]
            value = value - coef_ref[s * 5 + 1, i] * two[n] - coef_ref[s * 5, i] * one[n]
            f_ref[n, layer_at(i), :] = value
            new.append(value)
        return new, one

    start = ([zero] * 5, [zero] * 5)
    last = lax.fori_loop(0, cells, forward, start, unroll=UNROLL)
    first = lax.fori_loop(0, cells, swept_back(cells, f_ref, coef_ref), start, unroll=UNROLL)
    spread(out_ref, 0, lane, with_fifth(last + first))
    spread(out_ref, 6, lane, with_fifth(gives))
    spread(out_ref, 11, lane, [[-0.5 * dt_ref[pl.ds(i * 8, 8), :] for i in (0, 1, cells - 2, cells - 1)]])
    for quarter in range(4):
        out_ref[pl.ds(quarter * 8 * OUT + 5, 8, stride=OUT), :] = response


def beside_kernel(
    cells, f_in, dt_edge_ref, east_ref, west_ref, coef_ref, char_mat, f_ref, row_ref, sweep_ref
):
    sub, lane = iotas()
    scale = -0.5 * dt_edge_ref[...]
    beside = to_char(
        char_mat,
        [
            scale * jnp.where(sub < 4, -west_ref[pl.ds(v * 8, 8), :], east_ref[pl.ds(v * 8, 8), :])
            for v in range(5)
        ],
    )
    outside = outer(sub, lane)
    zero = jnp.where((lane < 0) & (sub < 0), 1.0, 0.0).astype(F32)

    def forward(i, carry):
        one, two = carry
        new = []
        for n, s in enumerate(SYSTEM):
            char = jnp.where(outside, roll(beside[n], (128 - i) % 128, 1), 0.0)
            value = coef_ref[s * 5 + 2, i] * char - coef_ref[s * 5 + 1, i] * two[n] - coef_ref[s * 5, i] * one[n]
            sweep_ref[n, layer_at(i), :] = value
            f_ref[n, layer_at(i), :] = f_in[n, layer_at(i), :] + value
            new.append(value)
        return new, one

    start = ([zero] * 5, [zero] * 5)
    last = lax.fori_loop(0, cells, forward, start, unroll=UNROLL)
    first = lax.fori_loop(0, cells, swept_back(cells, sweep_ref, coef_ref), start, unroll=UNROLL)
    ends = last + first
    row_ref[...] = jnp.zeros(TILE, F32)
    for pair in range(2):
        total = jnp.zeros(TILE, F32)
        for n in range(2):
            for u in range(5):
                value = jnp.sum(ends[pair * 2 + n][u], axis=1, keepdims=True)
                total = jnp.where(lane == n * 64 + u * 8 + sub, value, total)
        row_ref[pair : pair + 1, :] = jnp.sum(total, axis=0, keepdims=True)


def reduced_kernel(count, in_ref, row_ref, out_ref, edge_coef_ref, part_ref, coef_ref, four_ref):
    lane = lax.broadcasted_iota(jnp.int32, (count, 128), 1)
    place = lax.broadcasted_iota(jnp.int32, (count, 128), 0)

    def rows(n):
        return in_ref[pl.ds(n, count, stride=OUT), :]

    def put(n, value):
        out_ref[pl.ds(n, count, stride=BACK), :] = value

    response = rows(5)

    def wide(k, c):
        at = [(s * 4 + k) * 8 + c for s in range(3)]
        return [jnp.broadcast_to(response[:, n : n + 1], (count, 128)) for n in at]

    def factor(systems):
        return jnp.where(lane < 96, systems[0], systems[1]), systems[2]

    step, fifth = rows(11), rows(10)
    added = []
    for m in range(4):
        scales = by_quarter(lane, [quarter_move(step, m, u) for u in range(4)])
        pair = []
        for give, scale in ((rows(6 + m), scales), (quarter_move(fifth, m, 0), quarter_move(step, m, 0))):
            if m < 2:
                give = jnp.where(place == 0, 0.0, roll(give, 1, 0))
            else:
                give = jnp.where(place == count - 1, 0.0, roll(give, count - 1, 0))
            pair.append(scale * give)
        added.append(pair)
        put(5 + m, pair[0])
    put(9, by_quarter(lane, [quarter_move(added[m][1], 0, m) for m in range(4)]))
    fifth = rows(4)
    for k in range(4):
        values = [rows(k), quarter_move(fifth, k, 0)]
        for m in range(4):
            for tile, part in enumerate(factor(wide(k, 4 + m))):
                values[tile] = values[tile] + part * added[m][tile]
        for tile in range(2):
            part_ref[k, tile] = values[tile]
        for c in range(2 if k < 2 else 4):
            systems = wide(k, c)
            for tile, part in enumerate(factor(systems)):
                coef_ref[k * 4 + c, tile] = part
            edge_coef_ref[k * 4 + c] = jnp.where(
                lane < 24, systems[0], jnp.where(lane < 32, systems[1], systems[2])
            )
    for n in range(2):
        put(10 + n, jnp.broadcast_to(row_ref[n : n + 1, :], (count, 128)))
    zero = jnp.zeros((1, 128), F32)

    def take(ref, n, tile, t):
        return ref[n, tile, t : t + 1, :]

    inflow = [(zero, zero), (zero, zero)]
    sums = []
    for t in range(count):
        row = []
        for tile in range(2):
            one, two = inflow[tile]
            for k, value in ((0, one), (1, two)):
                if tile == 0:
                    out_ref[t * BACK + k : t * BACK + k + 1, :] = value
                else:
                    four_ref[k, t : t + 1, :] = value
            made = [
                take(part_ref, k, tile, t)
                + take(coef_ref, k * 4, tile, t) * one
                + take(coef_ref, k * 4 + 1, tile, t) * two
                for k in range(4)
            ]
            inflow[tile] = (made[0], made[1])
            row.append((made[2], made[3]))
        sums.append(row)
    inflow = [(zero, zero), (zero, zero)]
    for t in reversed(range(count)):
        for tile in range(2):
            one, two = inflow[tile]
            for k, value in ((2, one), (3, two)):
                if tile == 0:
                    out_ref[t * BACK + k : t * BACK + k + 1, :] = value
                else:
                    four_ref[k, t : t + 1, :] = value
            inflow[tile] = tuple(
                sums[t][tile][k - 2]
                + take(coef_ref, k * 4 + 2, tile, t) * one
                + take(coef_ref, k * 4 + 3, tile, t) * two
                for k in (2, 3)
            )
    put(4, by_quarter(lane, [quarter_move(four_ref[k], 0, k) for k in range(4)]))


def edge_inflow(count, in_ref, coef_ref, edge_ref, flow_ref):
    for pair in range(2):
        both = in_ref[pl.ds(10 + pair, count, stride=BACK), :]
        edge_ref[pair * 2] = both
        edge_ref[pair * 2 + 1] = roll(both, 64, 1)

    def take(k, c, t):
        return coef_ref[k * 4 + c, t : t + 1, :]

    zero = jnp.zeros((1, 128), F32)
    one, two = zero, zero
    sums = []
    for t in range(count):
        flow_ref[0, t : t + 1, :] = one
        flow_ref[1, t : t + 1, :] = two
        made = [edge_ref[k, t : t + 1, :] + take(k, 0, t) * one + take(k, 1, t) * two for k in range(4)]
        one, two = made[:2]
        sums.append(made[2:])
    one, two = zero, zero
    for t in reversed(range(count)):
        flow_ref[2, t : t + 1, :] = one
        flow_ref[3, t : t + 1, :] = two
        one, two = [sums[t][k - 2] + take(k, 2, t) * one + take(k, 3, t) * two for k in (2, 3)]


def final_kernel(cells, count, f_ref, in_ref, edge_coef_ref, coef_ref, cons_mat, out_ref, shift_ref, edge_ref, flow_ref):
    sub, lane = iotas()
    edge_inflow(count, in_ref, edge_coef_ref, edge_ref, flow_ref)
    place = lax.axis_index("sec")
    outside = outer(sub, lane)
    inflow = gathered(in_ref, 0, lane)
    for k in range(4):
        row = jnp.broadcast_to(flow_ref[k, pl.ds(place, 1), :], TILE)
        for u in range(5):
            value = jnp.sum(jnp.where(lane == u * 8 + sub, row, 0.0), axis=1, keepdims=True)
            inflow[k][u] = inflow[k][u] + jnp.where(outside, value, 0.0)
    added = gathered(in_ref, 5, lane)

    def forward(i, carry, right=None):
        one, two = carry
        new = []
        for n, s in enumerate(SYSTEM):
            value = -(coef_ref[s * 5 + 1, i] * two[n]) - coef_ref[s * 5, i] * one[n]
            if right is not None:
                value = value + coef_ref[s * 5 + 2, i] * right[n]
            shift_ref[n, layer_at(i), :] = f_ref[n, layer_at(i), :] + value
            new.append(value)
        return new, one

    last = (inflow[0], inflow[1])
    for i in (0, 1):
        last = forward(i, last, added[i])
    last = lax.fori_loop(2, cells - 2, forward, last, unroll=7)
    for i in (0, 1):
        last = forward(cells - 2 + i, last, added[2 + i])

    def backward(step, carry):
        i = cells - 1 - step
        one, two = carry
        new = [
            shift_ref[n, layer_at(i), :] - coef_ref[s * 5 + 4, i] * two[n] - coef_ref[s * 5 + 3, i] * one[n]
            for n, s in enumerate(SYSTEM)
        ]
        for n in range(5):
            out_ref[layer_at(n * cells + i), :] = sum(cons_mat[n, v] * new[v] for v in range(5))
        return new, one

    lax.fori_loop(0, cells, backward, (inflow[2], inflow[3]), unroll=UNROLL)


def shaped(*shape):
    return jax.ShapeDtypeStruct(shape, F32)


def kept(*shape):
    return pltpu.VMEM(shape, F32)


def near(x):
    return pltpu.with_memory_space_constraint(x, pltpu.VMEM)


def exchanged(x, count):
    chunks = x.reshape(count, 1, x.size // count)
    return lax.all_to_all(chunks, "sec", 0, 0, tiled=True).reshape(x.shape)


def near_scalars(x):
    return pltpu.with_memory_space_constraint(x, pltpu.SMEM)


VMEM = pl.BlockSpec(memory_space=pltpu.VMEM)
SMEM = pl.BlockSpec(memory_space=pltpu.SMEM)
ANY = pl.BlockSpec(memory_space=pl.ANY)


def on_device(state, time_step, to_char, to_cons, lower_bands, upper_bands):
    cells = state.shape[1]
    count = lax.axis_size("sec")
    columns = lax.axis_size("cross")
    flat = state.reshape(5, cells, 4, 2, 128).transpose(0, 1, 3, 2, 4).reshape(5 * cells * 8, 128)
    steps = time_step.reshape(cells, 4, 2, 128).transpose(0, 2, 1, 3).reshape(cells * 8, 128)
    block = (5, cells * 8, 128)
    ends, swept, padded, steps, coef, char_mat, cons_mat = pl.pallas_call(
        lambda *refs: own_kernel(cells, *refs),
        out_shape=(
            kept(count * OUT, 128),
            kept(*block),
            kept(5, (cells + 4) * 8, 128),
            kept(cells * 8, 128),
            pltpu.SMEM((16, 128), F32),
            pltpu.SMEM((5, 5), F32),
            pltpu.SMEM((5, 5), F32),
        ),
        in_specs=[ANY] * 6,
        out_specs=(VMEM,) * 4 + (SMEM,) * 3,
        scratch_shapes=[
            pltpu.VMEM(block, F32),
            pltpu.VMEM((3, cells * 8, 128), F32),
            pltpu.VMEM(lower_bands.shape, F32),
            pltpu.VMEM(upper_bands.shape, F32),
            pltpu.VMEM((16, 128), F32),
            pltpu.SemaphoreType.DMA((5,)),
            pltpu.SemaphoreType.DMA((6,)),
        ],
        name="own",
    )(flat, steps, lower_bands, upper_bands, to_char, to_cons)
    coef, char_mat, cons_mat = near_scalars(coef), near_scalars(char_mat), near_scalars(cons_mat)
    ends = exchanged(ends, count)
    edge, step_edge = pl.pallas_call(
        lambda *refs: edges_kernel(cells, *refs),
        out_shape=(kept(40, 128), kept(*TILE)),
        in_specs=[VMEM] * 2,
        out_specs=(VMEM, VMEM),
        name="edges",
    )(near(padded), near(steps))
    right = [(i, i + 1) for i in range(columns - 1)]
    west = near(lax.ppermute(edge, "cross", right))
    east = near(lax.ppermute(edge, "cross", [(j, i) for i, j in right]))
    swept, row = pl.pallas_call(
        lambda *refs: beside_kernel(cells, *refs),
        out_shape=(kept(*block), kept(*TILE)),
        in_specs=[VMEM] * 4 + [SMEM] * 2,
        out_specs=(VMEM, VMEM),
        scratch_shapes=[pltpu.VMEM(block, F32)],
        name="beside",
    )(near(swept), near(step_edge), east, west, coef, char_mat)
    inflow, edge_coef = pl.pallas_call(
        lambda *refs: reduced_kernel(count, *refs),
        out_shape=(kept(count * BACK, 128), kept(16, count, 128)),
        in_specs=[VMEM] * 2,
        out_specs=(VMEM, VMEM),
        scratch_shapes=[
            pltpu.VMEM((4, 2, count, 128), F32),
            pltpu.VMEM((16, 2, count, 128), F32),
            pltpu.VMEM((4, count, 128), F32),
        ],
        name="reduced",
    )(near(ends), near(row))
    inflow = exchanged(inflow, count)
    result = pl.pallas_call(
        lambda *refs: final_kernel(cells, count, *refs),
        out_shape=shaped(5 * cells * 8, 128),
        in_specs=[VMEM] * 3 + [SMEM] * 2,
        out_specs=VMEM,
        scratch_shapes=[
            pltpu.VMEM(block, F32),
            pltpu.VMEM((4, count, 128), F32),
            pltpu.VMEM((4, count, 128), F32),
        ],
        name="final",
    )(near(swept), near(inflow), near(edge_coef), coef, cons_mat)
    return result.reshape(5, cells, 2, 4, 128).transpose(0, 1, 3, 2, 4).reshape(state.shape)


def solution(mesh):
    in_specs = (
        P(None, "sec", None, "cross"),
        P("sec", None, "cross"),
        P(),
        P(),
        P(None, None, "sec"),
        P(None, None, "sec"),
    )
    out_specs = P(None, "sec", None, "cross")
    return jax.shard_map(
        on_device, mesh=mesh, in_specs=in_specs, out_specs=out_specs, check_vma=False
    )
```

```python
import jax
import jax.numpy as jnp
from jax import lax
from jax.experimental import pallas as pl
from jax.experimental.pallas import tpu as pltpu
from jax.sharding import PartitionSpec as P

SYSTEM = (0, 0, 0, 1, 2)
F32 = jnp.float32
OUT = 12
BACK = 12
PARTS = 2
STORES = 4
UNROLL = 32
TILE = (8, 128)


def iotas():
    sub = lax.broadcasted_iota(jnp.int32, TILE, 0)
    lane = lax.broadcasted_iota(jnp.int32, TILE, 1)
    return sub, lane


def roll(x, shift, axis):
    size = x.shape[axis]
    return pltpu.roll(x, shift % size if isinstance(shift, int) else shift, axis)


def primitives(q):
    inv = 1.0 / jnp.where(q[0] == 0.0, 1.0, q[0])
    kinetic = 0.5 * (q[1] * q[1] + q[2] * q[2] + q[3] * q[3]) * inv
    return inv, 0.4 * (q[4] - kinetic)


def flux(q, inv, pressure, k):
    velocity = q[1 + k] * inv
    parts = [q[1 + k], q[1] * velocity, q[2] * velocity, q[3] * velocity, (q[4] + pressure) * velocity]
    parts[1 + k] = parts[1 + k] + pressure
    return parts


def quarter_move(x, a, b):
    return x if a == b else roll(x, 32 * (b - a), 1)


def by_quarter(lane, xs):
    return jnp.where(
        lane < 64, jnp.where(lane < 32, xs[0], xs[1]), jnp.where(lane < 96, xs[2], xs[3])
    )


def packed_edges(cells, layer):
    sub, lane = iotas()
    total = jnp.zeros(TILE, F32)
    for i in range(cells):
        moved = roll(layer(i), i, 1) if i else layer(i)
        total = jnp.where(lane == jnp.where(sub < 4, i, (i - 1) % 128), moved, total)
    return total


def edges_kernel(cells, x_ref, dt_ref, edge_ref, dt_edge_ref):
    sub, _ = iotas()
    packed = []
    for v in range(5):
        total = packed_edges(cells, lambda i, v=v: x_ref[v, pl.ds(16 + i * 8, 8), :])
        total = roll(total, 4, 0)
        packed.append(jnp.where(sub < 4, roll(total, 1, 1), roll(total, 127, 1)))
    inv, pressure = primitives(packed)
    for v, part in enumerate(flux(packed, inv, pressure, 1)):
        edge_ref[pl.ds(v * 8, 8), :] = part
    dt_edge_ref[...] = packed_edges(cells, lambda i: dt_ref[pl.ds(i * 8, 8), :])


def layer_at(i):
    return pl.ds(i * 8 if isinstance(i, int) else pl.multiple_of(i * 8, 8), 8)


def to_char(char_mat, right):
    return [sum(char_mat[u, v] * right[v] for v in range(5)) for u in range(5)]


def spread(out_ref, row, lane, groups):
    for quarter in range(4):
        for k, four in enumerate(groups):
            out_ref[pl.ds(quarter * 8 * OUT + row + k, 8, stride=OUT), :] = by_quarter(
                lane, [quarter_move(four[u], quarter, u) for u in range(4)]
            )


def with_fifth(values):
    return [values[k][:4] for k in range(4)] + [[values[k][4] for k in range(4)]]


def gathered(in_ref, row, lane):
    values = []
    for k in range(5):
        parts = [in_ref[pl.ds(q * 8 * BACK + row + k, 8, stride=BACK), :] for q in range(4)]
        values.append(
            [by_quarter(lane, [quarter_move(parts[q], u, q) for q in range(4)]) for u in range(4)]
        )
    return [values[k] + [values[4][k]] for k in range(4)]


def outer(sub, lane):
    return (lane == jnp.where(sub < 4, 0, 127)) & (sub >= 0)


def swept_back(cells, f_ref, coef_ref):
    def backward(step, carry):
        i = cells - 1 - step
        one, two = carry
        new = [
            f_ref[n, layer_at(i), :] - coef_ref[s * 5 + 4, i] * two[n] - coef_ref[s * 5 + 3, i] * one[n]
            for n, s in enumerate(SYSTEM)
        ]
        return new, one

    return backward


def own_kernel(
    cells, x_hbm, dt_hbm, lower_hbm, upper_hbm, char_hbm, cons_hbm,
    out_ref, f_ref, x_ref, dt_ref, coef_ref, char_mat, cons_mat,
    char_ref, answer_ref, lower_ref, upper_ref, made_ref, x_sems, sems,
):
    sub, lane = iotas()
    rows = cells * 8
    part = rows // PARTS
    x_copies = [
        pltpu.make_async_copy(
            x_hbm.at[:, pl.ds(n * part, part)], x_ref.at[:, pl.ds(16 + n * part, part)], x_sems.at[n]
        )
        for n in range(PARTS)
    ]
    pairs = (
        (lower_hbm, lower_ref),
        (upper_hbm, upper_ref),
        (dt_hbm, dt_ref),
        (char_hbm, char_mat),
        (cons_hbm, cons_mat),
    )
    copies = [pltpu.make_async_copy(a, b, sems.at[n]) for n, (a, b) in enumerate(pairs)]
    for copy in copies[:2] + x_copies[:1] + copies[2:4] + x_copies[1:] + copies[4:]:
        copy.start()
    for v in range(5):
        x_ref[v, 0:16] = jnp.zeros((16, 128), F32)
        x_ref[v, pl.ds(16 + rows, 16)] = jnp.zeros((16, 128), F32)
    made_ref[...] = jnp.zeros(made_ref.shape, F32)
    copies[0].wait()
    copies[1].wait()
    for s in range(3):
        inverse = 1.0 / lower_ref[s, 2:3, :]
        made_ref[s * 5 : s * 5 + 1, 0:cells] = lower_ref[s, 1:2, :] * inverse
        made_ref[s * 5 + 1 : s * 5 + 2, 0:cells] = lower_ref[s, 0:1, :] * inverse
        made_ref[s * 5 + 2 : s * 5 + 3, 0:cells] = inverse
        made_ref[s * 5 + 3 : s * 5 + 5, 0:cells] = upper_ref[s]
    made = pltpu.make_async_copy(made_ref, coef_ref, sems.at[5])
    made.start()
    copies[2].wait()
    copies[3].wait()

    third = sub % 4

    def layer(i):
        return [x_ref[v, layer_at(i + 2), :] for v in range(5)]

    def line(i):
        q = layer(i)
        inv, pressure = primitives(q)
        return flux(q, inv, pressure, 0), inv, pressure

    def cell(i, carry):
        flux_before, (flux_now, inv, pressure) = carry
        q = layer(i)
        flux_after, inv_after, pressure_after = line(i + 1)
        side = flux(q, inv, pressure, 1)
        over = flux(q, inv, pressure, 2)
        two, one, next_one, next_two = (layer(i + n) for n in (-2, -1, 1, 2))
        scale = -0.5 * dt_ref[layer_at(i), :]
        right = []
        for v in range(5):
            down, up = roll(side[v], 1, 1), roll(side[v], 127, 1)
            cut = roll(jnp.where(lane == 0, down, up), 4, 0)
            cut = jnp.where((lane == 0) == (sub < 4), 0.0, cut)
            side_diff = jnp.where(lane == 127, cut, up) - jnp.where(lane == 0, cut, down)
            over_diff = jnp.where(third == 3, roll(over[v], 3, 0), roll(over[v], 7, 0)) - jnp.where(
                third == 0, roll(over[v], 5, 0), roll(over[v], 1, 0)
            )
            fourth = (two[v] + next_two[v]) - 4.0 * (one[v] + next_one[v]) + 6.0 * q[v]
            total = (flux_after[v] - flux_before[v]) + side_diff + over_diff + 0.125 * fourth
            right.append(scale * total)
        for u, value in enumerate(to_char(char_mat, right)):
            char_ref[u, layer_at(i), :] = value
        return flux_now, (flux_after, inv_after, pressure_after)

    begin = 0
    for n in range(PARTS):
        x_copies[n].wait()
        if n == 0:
            carry = (line(-1)[0], line(0))
        end = cells if n == PARTS - 1 else (n + 1) * cells // PARTS - 2
        carry = lax.fori_loop(begin, end, cell, carry, unroll=end - begin)
        begin = end
    copies[4].wait()
    made.wait()
    top, bottom = line(0), line(cells - 1)
    first_two, last_two = (layer(0), layer(1)), (layer(cells - 2), layer(cells - 1))
    gives = (
        [0.125 * (last_two[0][v] - 4.0 * last_two[1][v]) - bottom[0][v] for v in range(5)],
        [0.125 * last_two[1][v] for v in range(5)],
        [0.125 * first_two[0][v] for v in range(5)],
        [0.125 * (first_two[1][v] - 4.0 * first_two[0][v]) + top[0][v] for v in range(5)],
    )
    gives = [to_char(char_mat, give) for give in gives]

    unit = [jnp.where((lane == n) & (sub >= 0), 1.0, 0.0).astype(F32) for n in range(8)]
    zero = jnp.where((lane < 0) & (sub < 0), 1.0, 0.0).astype(F32)

    def forward(i, carry, right=None):
        one, two = carry
        new = []
        for n, s in enumerate(SYSTEM + (0, 1, 2)):
            value = -(coef_ref[s * 5 + 1, i] * two[n])
            if n < 5:
                value = coef_ref[s * 5 + 2, i] * char_ref[n, layer_at(i), :] + value
            elif right is not None:
                value = coef_ref[s * 5 + 2, i] * right + value
            value = value - coef_ref[s * 5, i] * one[n]
            if n < 5:
                f_ref[n, layer_at(i), :] = value
            else:
                answer_ref[n - 5, layer_at(i), :] = value
            new.append(value)
        return new, one

    def backward(step, carry):
        i = cells - 1 - step
        one, two = carry
        new = []
        for n, s in enumerate(SYSTEM + (0, 1, 2)):
            value = f_ref[n, layer_at(i), :] if n < 5 else answer_ref[n - 5, layer_at(i), :]
            new.append(value - coef_ref[s * 5 + 4, i] * two[n] - coef_ref[s * 5 + 3, i] * one[n])
        return new, one

    start = [zero] * 5
    last = (start + [unit[0]] * 3, start + [unit[1]] * 3)
    for i in (0, 1):
        last = forward(i, last, unit[4 + i])
    last = lax.fori_loop(2, cells - 2, forward, last, unroll=cells - 4)
    for i in (0, 1):
        last = forward(cells - 2 + i, last, unit[6 + i])
    first = lax.fori_loop(0, cells, backward, (start + [unit[2]] * 3, start + [unit[3]] * 3), unroll=UNROLL)
    ends = last + first
    response = jnp.zeros(TILE, F32)
    for s in range(3):
        for k in range(4):
            at = (s * 4 + k) * 8
            moved = ends[k][5 + s] if at == 0 else roll(ends[k][5 + s], at, 1)
            response = jnp.where((lane >= at) & (lane < at + 8), moved, response)
    response = jnp.broadcast_to(response[0:1, :], TILE)
    spread(out_ref, 0, lane, with_fifth(ends))
    spread(out_ref, 6, lane, with_fifth(gives))
    spread(out_ref, 11, lane, [[-0.5 * dt_ref[pl.ds(i * 8, 8), :] for i in (0, 1, cells - 2, cells - 1)]])
    for quarter in range(4):
        out_ref[pl.ds(quarter * 8 * OUT + 5, 8, stride=OUT), :] = response


def beside_kernel(
    cells, f_in, dt_edge_ref, east_ref, west_ref, coef_ref, char_mat, f_ref, row_ref, sweep_ref
):
    sub, lane = iotas()
    scale = -0.5 * dt_edge_ref[...]
    beside = to_char(
        char_mat,
        [
            scale * jnp.where(sub < 4, -west_ref[pl.ds(v * 8, 8), :], east_ref[pl.ds(v * 8, 8), :])
            for v in range(5)
        ],
    )
    outside = outer(sub, lane)
    zero = jnp.where((lane < 0) & (sub < 0), 1.0, 0.0).astype(F32)

    def forward(i, carry):
        one, two = carry
        new = []
        for n, s in enumerate(SYSTEM):
            char = jnp.where(outside, roll(beside[n], (128 - i) % 128, 1), 0.0)
            value = coef_ref[s * 5 + 2, i] * char - coef_ref[s * 5 + 1, i] * two[n] - coef_ref[s * 5, i] * one[n]
            sweep_ref[n, layer_at(i), :] = value
            f_ref[n, layer_at(i), :] = f_in[n, layer_at(i), :] + value
            new.append(value)
        return new, one

    start = ([zero] * 5, [zero] * 5)
    last = lax.fori_loop(0, cells, forward, start, unroll=UNROLL)
    first = lax.fori_loop(0, cells, swept_back(cells, sweep_ref, coef_ref), start, unroll=UNROLL)
    ends = last + first
    row_ref[...] = jnp.zeros(TILE, F32)
    for pair in range(2):
        total = jnp.zeros(TILE, F32)
        for n in range(2):
            for u in range(5):
                value = jnp.sum(ends[pair * 2 + n][u], axis=1, keepdims=True)
                total = jnp.where(lane == n * 64 + u * 8 + sub, value, total)
        row_ref[pair : pair + 1, :] = jnp.sum(total, axis=0, keepdims=True)


def reduced_kernel(count, in_ref, row_ref, out_ref, edge_coef_ref, part_ref, coef_ref, four_ref):
    lane = lax.broadcasted_iota(jnp.int32, (count, 128), 1)
    place = lax.broadcasted_iota(jnp.int32, (count, 128), 0)

    def rows(n):
        return in_ref[pl.ds(n, count, stride=OUT), :]

    def put(n, value):
        out_ref[pl.ds(n, count, stride=BACK), :] = value

    response = rows(5)

    def wide(k, c):
        at = [(s * 4 + k) * 8 + c for s in range(3)]
        return [jnp.broadcast_to(response[:, n : n + 1], (count, 128)) for n in at]

    def factor(systems):
        return jnp.where(lane < 96, systems[0], systems[1]), systems[2]

    step, fifth = rows(11), rows(10)
    added = []
    for m in range(4):
        scales = by_quarter(lane, [quarter_move(step, m, u) for u in range(4)])
        pair = []
        for give, scale in ((rows(6 + m), scales), (quarter_move(fifth, m, 0), quarter_move(step, m, 0))):
            if m < 2:
                give = jnp.where(place == 0, 0.0, roll(give, 1, 0))
            else:
                give = jnp.where(place == count - 1, 0.0, roll(give, count - 1, 0))
            pair.append(scale * give)
        added.append(pair)
        put(5 + m, pair[0])
    put(9, by_quarter(lane, [quarter_move(added[m][1], 0, m) for m in range(4)]))
    fifth = rows(4)
    for k in range(4):
        values = [rows(k), quarter_move(fifth, k, 0)]
        for m in range(4):
            for tile, part in enumerate(factor(wide(k, 4 + m))):
                values[tile] = values[tile] + part * added[m][tile]
        for tile in range(2):
            part_ref[k, tile] = values[tile]
        for c in range(2 if k < 2 else 4):
            systems = wide(k, c)
            for tile, part in enumerate(factor(systems)):
                coef_ref[k * 4 + c, tile] = part
            edge_coef_ref[k * 4 + c] = jnp.where(
                lane < 24, systems[0], jnp.where(lane < 32, systems[1], systems[2])
            )
    for n in range(2):
        put(10 + n, jnp.broadcast_to(row_ref[n : n + 1, :], (count, 128)))
    zero = jnp.zeros((1, 128), F32)

    def take(ref, n, tile, t):
        return ref[n, tile, t : t + 1, :]

    inflow = [(zero, zero), (zero, zero)]
    sums = []
    for t in range(count):
        row = []
        for tile in range(2):
            one, two = inflow[tile]
            for k, value in ((0, one), (1, two)):
                if tile == 0:
                    out_ref[t * BACK + k : t * BACK + k + 1, :] = value
                else:
                    four_ref[k, t : t + 1, :] = value
            made = [
                take(part_ref, k, tile, t)
                + take(coef_ref, k * 4, tile, t) * one
                + take(coef_ref, k * 4 + 1, tile, t) * two
                for k in range(4)
            ]
            inflow[tile] = (made[0], made[1])
            row.append((made[2], made[3]))
        sums.append(row)
    inflow = [(zero, zero), (zero, zero)]
    for t in reversed(range(count)):
        for tile in range(2):
            one, two = inflow[tile]
            for k, value in ((2, one), (3, two)):
                if tile == 0:
                    out_ref[t * BACK + k : t * BACK + k + 1, :] = value
                else:
                    four_ref[k, t : t + 1, :] = value
            inflow[tile] = tuple(
                sums[t][tile][k - 2]
                + take(coef_ref, k * 4 + 2, tile, t) * one
                + take(coef_ref, k * 4 + 3, tile, t) * two
                for k in (2, 3)
            )
    put(4, by_quarter(lane, [quarter_move(four_ref[k], 0, k) for k in range(4)]))


def edge_inflow(count, in_ref, coef_ref, edge_ref, flow_ref):
    for pair in range(2):
        both = in_ref[pl.ds(10 + pair, count, stride=BACK), :]
        edge_ref[pair * 2] = both
        edge_ref[pair * 2 + 1] = roll(both, 64, 1)

    def take(k, c, t):
        return coef_ref[k * 4 + c, t : t + 1, :]

    zero = jnp.zeros((1, 128), F32)
    one, two = zero, zero
    sums = []
    for t in range(count):
        flow_ref[0, t : t + 1, :] = one
        flow_ref[1, t : t + 1, :] = two
        made = [edge_ref[k, t : t + 1, :] + take(k, 0, t) * one + take(k, 1, t) * two for k in range(4)]
        one, two = made[:2]
        sums.append(made[2:])
    one, two = zero, zero
    for t in reversed(range(count)):
        flow_ref[2, t : t + 1, :] = one
        flow_ref[3, t : t + 1, :] = two
        one, two = [sums[t][k - 2] + take(k, 2, t) * one + take(k, 3, t) * two for k in (2, 3)]


def final_kernel(
    cells, count, f_ref, in_ref, edge_coef_ref, coef_ref, cons_mat, out_hbm, shift_ref, edge_ref, flow_ref, made_ref, sems
):
    sub, lane = iotas()
    edge_inflow(count, in_ref, edge_coef_ref, edge_ref, flow_ref)
    place = lax.axis_index("sec")
    outside = outer(sub, lane)
    inflow = gathered(in_ref, 0, lane)
    for k in range(4):
        row = jnp.broadcast_to(flow_ref[k, pl.ds(place, 1), :], TILE)
        for u in range(5):
            value = jnp.sum(jnp.where(lane == u * 8 + sub, row, 0.0), axis=1, keepdims=True)
            inflow[k][u] = inflow[k][u] + jnp.where(outside, value, 0.0)
    added = gathered(in_ref, 5, lane)

    def forward(i, carry, right=None):
        one, two = carry
        new = []
        for n, s in enumerate(SYSTEM):
            value = -(coef_ref[s * 5 + 1, i] * two[n]) - coef_ref[s * 5, i] * one[n]
            if right is not None:
                value = value + coef_ref[s * 5 + 2, i] * right[n]
            shift_ref[n, layer_at(i), :] = f_ref[n, layer_at(i), :] + value
            new.append(value)
        return new, one

    last = (inflow[0], inflow[1])
    for i in (0, 1):
        last = forward(i, last, added[i])
    last = lax.fori_loop(2, cells - 2, forward, last, unroll=7)
    for i in (0, 1):
        last = forward(cells - 2 + i, last, added[2 + i])

    def backward(step, carry):
        i = cells - 1 - step
        one, two = carry
        new = [
            shift_ref[n, layer_at(i), :] - coef_ref[s * 5 + 4, i] * two[n] - coef_ref[s * 5 + 3, i] * one[n]
            for n, s in enumerate(SYSTEM)
        ]
        for n in range(5):
            made_ref[n, layer_at(i), :] = sum(cons_mat[n, v] * new[v] for v in range(5))
        return new, one

    carry = (inflow[2], inflow[3])
    part = cells // STORES
    copies = []
    for p in range(STORES):
        carry = lax.fori_loop(p * part, (p + 1) * part, backward, carry, unroll=part)
        at = pl.ds((cells - (p + 1) * part) * 8, part * 8)
        copies.append(pltpu.make_async_copy(made_ref.at[:, at], out_hbm.at[:, at], sems.at[p]))
        copies[-1].start()
    for copy in copies:
        copy.wait()


def shaped(*shape):
    return jax.ShapeDtypeStruct(shape, F32)


def kept(*shape):
    return pltpu.VMEM(shape, F32)


def near(x):
    return pltpu.with_memory_space_constraint(x, pltpu.VMEM)


def exchanged(x, count):
    chunks = x.reshape(count, 1, x.size // count)
    return lax.all_to_all(chunks, "sec", 0, 0, tiled=True).reshape(x.shape)


def near_scalars(x):
    return pltpu.with_memory_space_constraint(x, pltpu.SMEM)


VMEM = pl.BlockSpec(memory_space=pltpu.VMEM)
SMEM = pl.BlockSpec(memory_space=pltpu.SMEM)
ANY = pl.BlockSpec(memory_space=pl.ANY)


def on_device(state, time_step, to_char, to_cons, lower_bands, upper_bands):
    cells = state.shape[1]
    count = lax.axis_size("sec")
    columns = lax.axis_size("cross")
    flat = state.reshape(5, cells, 4, 2, 128).transpose(0, 1, 3, 2, 4).reshape(5, cells * 8, 128)
    steps = time_step.reshape(cells, 4, 2, 128).transpose(0, 2, 1, 3).reshape(cells * 8, 128)
    block = (5, cells * 8, 128)
    ends, swept, padded, steps, coef, char_mat, cons_mat = pl.pallas_call(
        lambda *refs: own_kernel(cells, *refs),
        out_shape=(
            kept(count * OUT, 128),
            kept(*block),
            kept(5, (cells + 4) * 8, 128),
            kept(cells * 8, 128),
            pltpu.SMEM((16, 128), F32),
            pltpu.SMEM((5, 5), F32),
            pltpu.SMEM((5, 5), F32),
        ),
        in_specs=[ANY] * 6,
        out_specs=(VMEM,) * 4 + (SMEM,) * 3,
        scratch_shapes=[
            pltpu.VMEM(block, F32),
            pltpu.VMEM((3, cells * 8, 128), F32),
            pltpu.VMEM(lower_bands.shape, F32),
            pltpu.VMEM(upper_bands.shape, F32),
            pltpu.VMEM((16, 128), F32),
            pltpu.SemaphoreType.DMA((PARTS,)),
            pltpu.SemaphoreType.DMA((6,)),
        ],
        name="own",
    )(flat, steps, lower_bands, upper_bands, to_char, to_cons)
    coef, char_mat, cons_mat = near_scalars(coef), near_scalars(char_mat), near_scalars(cons_mat)
    ends = exchanged(ends, count)
    edge, step_edge = pl.pallas_call(
        lambda *refs: edges_kernel(cells, *refs),
        out_shape=(kept(40, 128), kept(*TILE)),
        in_specs=[VMEM] * 2,
        out_specs=(VMEM, VMEM),
        name="edges",
    )(near(padded), near(steps))
    right = [(i, i + 1) for i in range(columns - 1)]
    west = near(lax.ppermute(edge, "cross", right))
    east = near(lax.ppermute(edge, "cross", [(j, i) for i, j in right]))
    swept, row = pl.pallas_call(
        lambda *refs: beside_kernel(cells, *refs),
        out_shape=(kept(*block), kept(*TILE)),
        in_specs=[VMEM] * 4 + [SMEM] * 2,
        out_specs=(VMEM, VMEM),
        scratch_shapes=[pltpu.VMEM(block, F32)],
        name="beside",
    )(near(swept), near(step_edge), east, west, coef, char_mat)
    inflow, edge_coef = pl.pallas_call(
        lambda *refs: reduced_kernel(count, *refs),
        out_shape=(kept(count * BACK, 128), kept(16, count, 128)),
        in_specs=[VMEM] * 2,
        out_specs=(VMEM, VMEM),
        scratch_shapes=[
            pltpu.VMEM((4, 2, count, 128), F32),
            pltpu.VMEM((16, 2, count, 128), F32),
            pltpu.VMEM((4, count, 128), F32),
        ],
        name="reduced",
    )(near(ends), near(row))
    inflow = exchanged(inflow, count)
    result = pl.pallas_call(
        lambda *refs: final_kernel(cells, count, *refs),
        out_shape=shaped(*block),
        in_specs=[VMEM] * 3 + [SMEM] * 2,
        out_specs=ANY,
        scratch_shapes=[
            pltpu.VMEM(block, F32),
            pltpu.VMEM((4, count, 128), F32),
            pltpu.VMEM((4, count, 128), F32),
            pltpu.VMEM(block, F32),
            pltpu.SemaphoreType.DMA((STORES,)),
        ],
        name="final",
    )(near(swept), near(inflow), near(edge_coef), coef, cons_mat)
    return result.reshape(5, cells, 2, 4, 128).transpose(0, 1, 3, 2, 4).reshape(state.shape)


def solution(mesh):
    in_specs = (
        P(None, "sec", None, "cross"),
        P("sec", None, "cross"),
        P(),
        P(),
        P(None, None, "sec"),
        P(None, None, "sec"),
    )
    out_specs = P(None, "sec", None, "cross")
    return jax.shard_map(
        on_device, mesh=mesh, in_specs=in_specs, out_specs=out_specs, check_vma=False
    )
```

```python
import jax
import jax.numpy as jnp
from jax import lax
from jax.experimental import pallas as pl
from jax.experimental.pallas import tpu as pltpu
from jax.sharding import PartitionSpec as P

SYSTEM = (0, 0, 0, 1, 2)
F32 = jnp.float32
OUT = 12
BACK = 12
PARTS = 2
STORES = 4
UNROLL = 32
TILE = (8, 128)


def iotas():
    sub = lax.broadcasted_iota(jnp.int32, TILE, 0)
    lane = lax.broadcasted_iota(jnp.int32, TILE, 1)
    return sub, lane


def roll(x, shift, axis):
    size = x.shape[axis]
    return pltpu.roll(x, shift % size if isinstance(shift, int) else shift, axis)


def primitives(q):
    inv = 1.0 / jnp.where(q[0] == 0.0, 1.0, q[0])
    kinetic = 0.5 * (q[1] * q[1] + q[2] * q[2] + q[3] * q[3]) * inv
    return inv, 0.4 * (q[4] - kinetic)


def flux(q, inv, pressure, k):
    velocity = q[1 + k] * inv
    parts = [q[1 + k], q[1] * velocity, q[2] * velocity, q[3] * velocity, (q[4] + pressure) * velocity]
    parts[1 + k] = parts[1 + k] + pressure
    return parts


def quarter_move(x, a, b):
    return x if a == b else roll(x, 32 * (b - a), 1)


def by_quarter(lane, xs):
    return jnp.where(
        lane < 64, jnp.where(lane < 32, xs[0], xs[1]), jnp.where(lane < 96, xs[2], xs[3])
    )


def packed_edges(cells, layer):
    sub, lane = iotas()
    total = jnp.zeros(TILE, F32)
    for i in range(cells):
        moved = roll(layer(i), i, 1) if i else layer(i)
        total = jnp.where(lane == jnp.where(sub < 4, i, (i - 1) % 128), moved, total)
    return total


def edges_kernel(cells, x_ref, dt_ref, edge_ref, dt_edge_ref):
    sub, _ = iotas()
    packed = []
    for v in range(5):
        total = packed_edges(cells, lambda i, v=v: x_ref[v, pl.ds(16 + i * 8, 8), :])
        total = roll(total, 4, 0)
        packed.append(jnp.where(sub < 4, roll(total, 1, 1), roll(total, 127, 1)))
    inv, pressure = primitives(packed)
    for v, part in enumerate(flux(packed, inv, pressure, 1)):
        edge_ref[pl.ds(v * 8, 8), :] = part
    dt_edge_ref[...] = packed_edges(cells, lambda i: dt_ref[pl.ds(i * 8, 8), :])


def layer_at(i):
    return pl.ds(i * 8 if isinstance(i, int) else pl.multiple_of(i * 8, 8), 8)


def to_char(char_mat, right):
    return [sum(char_mat[u, v] * right[v] for v in range(5)) for u in range(5)]


def spread(out_ref, row, lane, groups):
    for quarter in range(4):
        for k, four in enumerate(groups):
            out_ref[pl.ds(quarter * 8 * OUT + row + k, 8, stride=OUT), :] = by_quarter(
                lane, [quarter_move(four[u], quarter, u) for u in range(4)]
            )


def with_fifth(values):
    return [values[k][:4] for k in range(4)] + [[values[k][4] for k in range(4)]]


def gathered(in_ref, row, lane):
    values = []
    for k in range(5):
        parts = [in_ref[pl.ds(q * 8 * BACK + row + k, 8, stride=BACK), :] for q in range(4)]
        values.append(
            [by_quarter(lane, [quarter_move(parts[q], u, q) for q in range(4)]) for u in range(4)]
        )
    return [values[k] + [values[4][k]] for k in range(4)]


def outer(sub, lane):
    return (lane == jnp.where(sub < 4, 0, 127)) & (sub >= 0)


def swept_back(cells, f_ref, coef_ref):
    def backward(step, carry):
        i = cells - 1 - step
        one, two = carry
        new = [
            f_ref[n, layer_at(i), :] - coef_ref[s * 5 + 4, i] * two[n] - coef_ref[s * 5 + 3, i] * one[n]
            for n, s in enumerate(SYSTEM)
        ]
        return new, one

    return backward


def own_kernel(
    cells, x_hbm, dt_hbm, lower_hbm, upper_hbm, char_hbm, cons_hbm,
    out_ref, f_ref, x_ref, dt_ref, coef_ref, char_mat, cons_mat,
    char_ref, answer_ref, lower_ref, upper_ref, made_ref, x_sems, sems,
):
    sub, lane = iotas()
    rows = cells * 8
    part = rows // PARTS
    x_copies = [
        pltpu.make_async_copy(
            x_hbm.at[:, pl.ds(n * part, part)], x_ref.at[:, pl.ds(16 + n * part, part)], x_sems.at[n]
        )
        for n in range(PARTS)
    ]
    pairs = (
        (lower_hbm, lower_ref),
        (upper_hbm, upper_ref),
        (dt_hbm, dt_ref),
        (char_hbm, char_mat),
        (cons_hbm, cons_mat),
    )
    copies = [pltpu.make_async_copy(a, b, sems.at[n]) for n, (a, b) in enumerate(pairs)]
    for copy in copies[:2] + x_copies[:1] + copies[2:4] + x_copies[1:] + copies[4:]:
        copy.start()
    for v in range(5):
        x_ref[v, 0:16] = jnp.zeros((16, 128), F32)
        x_ref[v, pl.ds(16 + rows, 16)] = jnp.zeros((16, 128), F32)
    made_ref[...] = jnp.zeros(made_ref.shape, F32)
    copies[0].wait()
    copies[1].wait()
    for s in range(3):
        inverse = 1.0 / lower_ref[s, 2:3, :]
        made_ref[s * 5 : s * 5 + 1, 0:cells] = lower_ref[s, 1:2, :] * inverse
        made_ref[s * 5 + 1 : s * 5 + 2, 0:cells] = lower_ref[s, 0:1, :] * inverse
        made_ref[s * 5 + 2 : s * 5 + 3, 0:cells] = inverse
        made_ref[s * 5 + 3 : s * 5 + 5, 0:cells] = upper_ref[s]
    made = pltpu.make_async_copy(made_ref, coef_ref, sems.at[5])
    made.start()
    copies[2].wait()
    copies[3].wait()

    third = sub % 4

    def layer(i):
        return [x_ref[v, layer_at(i + 2), :] for v in range(5)]

    def line(i):
        q = layer(i)
        inv, pressure = primitives(q)
        return flux(q, inv, pressure, 0), inv, pressure

    def cell(i, carry):
        flux_before, (flux_now, inv, pressure) = carry
        q = layer(i)
        flux_after, inv_after, pressure_after = line(i + 1)
        side = flux(q, inv, pressure, 1)
        over = flux(q, inv, pressure, 2)
        two, one, next_one, next_two = (layer(i + n) for n in (-2, -1, 1, 2))
        scale = -0.5 * dt_ref[layer_at(i), :]
        right = []
        for v in range(5):
            down, up = roll(side[v], 1, 1), roll(side[v], 127, 1)
            cut = roll(jnp.where(lane == 0, down, up), 4, 0)
            cut = jnp.where((lane == 0) == (sub < 4), 0.0, cut)
            side_diff = jnp.where(lane == 127, cut, up) - jnp.where(lane == 0, cut, down)
            over_diff = jnp.where(third == 3, roll(over[v], 3, 0), roll(over[v], 7, 0)) - jnp.where(
                third == 0, roll(over[v], 5, 0), roll(over[v], 1, 0)
            )
            fourth = (two[v] + next_two[v]) - 4.0 * (one[v] + next_one[v]) + 6.0 * q[v]
            total = (flux_after[v] - flux_before[v]) + side_diff + over_diff + 0.125 * fourth
            right.append(scale * total)
        for u, value in enumerate(to_char(char_mat, right)):
            char_ref[u, layer_at(i), :] = value
        return flux_now, (flux_after, inv_after, pressure_after)

    begin = 0
    for n in range(PARTS):
        x_copies[n].wait()
        if n == 0:
            carry = (line(-1)[0], line(0))
        end = cells if n == PARTS - 1 else (n + 1) * cells // PARTS - 2
        carry = lax.fori_loop(begin, end, cell, carry, unroll=end - begin)
        begin = end
    copies[4].wait()
    made.wait()
    top, bottom = line(0), line(cells - 1)
    first_two, last_two = (layer(0), layer(1)), (layer(cells - 2), layer(cells - 1))
    gives = (
        [0.125 * (last_two[0][v] - 4.0 * last_two[1][v]) - bottom[0][v] for v in range(5)],
        [0.125 * last_two[1][v] for v in range(5)],
        [0.125 * first_two[0][v] for v in range(5)],
        [0.125 * (first_two[1][v] - 4.0 * first_two[0][v]) + top[0][v] for v in range(5)],
    )
    gives = [to_char(char_mat, give) for give in gives]

    unit = [jnp.where((lane == n) & (sub >= 0), 1.0, 0.0).astype(F32) for n in range(8)]
    zero = jnp.where((lane < 0) & (sub < 0), 1.0, 0.0).astype(F32)

    def forward(i, carry, right=None):
        one, two = carry
        new = []
        for n, s in enumerate(SYSTEM + (0, 1, 2)):
            value = -(coef_ref[s * 5 + 1, i] * two[n])
            if n < 5:
                value = coef_ref[s * 5 + 2, i] * char_ref[n, layer_at(i), :] + value
            elif right is not None:
                value = coef_ref[s * 5 + 2, i] * right + value
            value = value - coef_ref[s * 5, i] * one[n]
            if n < 5:
                f_ref[n, layer_at(i), :] = value
            else:
                answer_ref[n - 5, layer_at(i), :] = value
            new.append(value)
        return new, one

    def backward(step, carry):
        i = cells - 1 - step
        one, two = carry
        new = []
        for n, s in enumerate(SYSTEM + (0, 1, 2)):
            value = f_ref[n, layer_at(i), :] if n < 5 else answer_ref[n - 5, layer_at(i), :]
            new.append(value - coef_ref[s * 5 + 4, i] * two[n] - coef_ref[s * 5 + 3, i] * one[n])
        return new, one

    start = [zero] * 5
    last = (start + [unit[0]] * 3, start + [unit[1]] * 3)
    for i in (0, 1):
        last = forward(i, last, unit[4 + i])
    last = lax.fori_loop(2, cells - 2, forward, last, unroll=cells - 4)
    for i in (0, 1):
        last = forward(cells - 2 + i, last, unit[6 + i])
    first = lax.fori_loop(0, cells, backward, (start + [unit[2]] * 3, start + [unit[3]] * 3), unroll=UNROLL)
    ends = last + first
    response = jnp.zeros(TILE, F32)
    for s in range(3):
        for k in range(4):
            at = (s * 4 + k) * 8
            moved = ends[k][5 + s] if at == 0 else roll(ends[k][5 + s], at, 1)
            response = jnp.where((lane >= at) & (lane < at + 8), moved, response)
    response = jnp.broadcast_to(response[0:1, :], TILE)
    spread(out_ref, 0, lane, with_fifth(ends))
    spread(out_ref, 6, lane, with_fifth(gives))
    spread(out_ref, 11, lane, [[-0.5 * dt_ref[pl.ds(i * 8, 8), :] for i in (0, 1, cells - 2, cells - 1)]])
    for quarter in range(4):
        out_ref[pl.ds(quarter * 8 * OUT + 5, 8, stride=OUT), :] = response


def reduced_kernel(
    cells, count, in_ref, f_in, dt_edge_ref, west_ref, east_ref, scalars, char_mat,
    out_ref, edge_coef_ref, f_ref, part_ref, coef_ref, four_ref, sweep_ref,
):
    lane = lax.broadcasted_iota(jnp.int32, (count, 128), 1)
    place = lax.broadcasted_iota(jnp.int32, (count, 128), 0)

    def rows(n):
        return in_ref[pl.ds(n, count, stride=OUT), :]

    def put(n, value):
        out_ref[pl.ds(n, count, stride=BACK), :] = value

    response = rows(5)

    def wide(k, c):
        at = [(s * 4 + k) * 8 + c for s in range(3)]
        return [jnp.broadcast_to(response[:, n : n + 1], (count, 128)) for n in at]

    def factor(systems):
        return jnp.where(lane < 96, systems[0], systems[1]), systems[2]

    step, fifth = rows(11), rows(10)
    added = []
    for m in range(4):
        scales = by_quarter(lane, [quarter_move(step, m, u) for u in range(4)])
        pair = []
        for give, scale in ((rows(6 + m), scales), (quarter_move(fifth, m, 0), quarter_move(step, m, 0))):
            if m < 2:
                give = jnp.where(place == 0, 0.0, roll(give, 1, 0))
            else:
                give = jnp.where(place == count - 1, 0.0, roll(give, count - 1, 0))
            pair.append(scale * give)
        added.append(pair)
        put(5 + m, pair[0])
    put(9, by_quarter(lane, [quarter_move(added[m][1], 0, m) for m in range(4)]))
    fifth = rows(4)
    for k in range(4):
        values = [rows(k), quarter_move(fifth, k, 0)]
        for m in range(4):
            for tile, part in enumerate(factor(wide(k, 4 + m))):
                values[tile] = values[tile] + part * added[m][tile]
        for tile in range(2):
            part_ref[k, tile] = values[tile]
        for c in range(2 if k < 2 else 4):
            systems = wide(k, c)
            for tile, part in enumerate(factor(systems)):
                coef_ref[k * 4 + c, tile] = part
            edge_coef_ref[k * 4 + c] = jnp.where(
                lane < 24, systems[0], jnp.where(lane < 32, systems[1], systems[2])
            )
    sub, tile_lane = iotas()
    scale = -0.5 * dt_edge_ref[...]
    beside = to_char(
        char_mat,
        [
            scale * jnp.where(sub < 4, -west_ref[pl.ds(v * 8, 8), :], east_ref[pl.ds(v * 8, 8), :])
            for v in range(5)
        ],
    )
    outside = outer(sub, tile_lane)

    def forward(i, carry):
        one, two = carry
        new = []
        for n, s in enumerate(SYSTEM):
            char = jnp.where(outside, roll(beside[n], (128 - i) % 128, 1), 0.0)
            value = scalars[s * 5 + 2, i] * char - scalars[s * 5 + 1, i] * two[n] - scalars[s * 5, i] * one[n]
            sweep_ref[n, layer_at(i), :] = value
            f_ref[n, layer_at(i), :] = f_in[n, layer_at(i), :] + value
            new.append(value)
        return new, one

    backward = swept_back(cells, sweep_ref, scalars)
    blank = jnp.zeros(TILE, F32)
    zero = jnp.zeros((1, 128), F32)

    def take(ref, n, tile, t):
        return ref[n, tile, t : t + 1, :]

    inflow = [(zero, zero), (zero, zero)]
    sums = []
    last = ([blank] * 5, [blank] * 5)
    for t in range(count):
        for i in range(t * cells // count, (t + 1) * cells // count):
            last = forward(i, last)
        row = []
        for tile in range(2):
            one, two = inflow[tile]
            for k, value in ((0, one), (1, two)):
                if tile == 0:
                    out_ref[t * BACK + k : t * BACK + k + 1, :] = value
                else:
                    four_ref[k, t : t + 1, :] = value
            made = [
                take(part_ref, k, tile, t)
                + take(coef_ref, k * 4, tile, t) * one
                + take(coef_ref, k * 4 + 1, tile, t) * two
                for k in range(4)
            ]
            inflow[tile] = (made[0], made[1])
            row.append((made[2], made[3]))
        sums.append(row)
    inflow = [(zero, zero), (zero, zero)]
    first = ([blank] * 5, [blank] * 5)
    for t in reversed(range(count)):
        for i in reversed(range(t * cells // count, (t + 1) * cells // count)):
            first = backward(cells - 1 - i, first)
        for tile in range(2):
            one, two = inflow[tile]
            for k, value in ((2, one), (3, two)):
                if tile == 0:
                    out_ref[t * BACK + k : t * BACK + k + 1, :] = value
                else:
                    four_ref[k, t : t + 1, :] = value
            inflow[tile] = tuple(
                sums[t][tile][k - 2]
                + take(coef_ref, k * 4 + 2, tile, t) * one
                + take(coef_ref, k * 4 + 3, tile, t) * two
                for k in (2, 3)
            )
    put(4, by_quarter(lane, [quarter_move(four_ref[k], 0, k) for k in range(4)]))
    ends = last + first
    for pair in range(2):
        total = blank
        for n in range(2):
            for u in range(5):
                value = jnp.sum(ends[pair * 2 + n][u], axis=1, keepdims=True)
                total = jnp.where(tile_lane == n * 64 + u * 8 + sub, value, total)
        put(10 + pair, jnp.broadcast_to(jnp.sum(total, axis=0, keepdims=True), (count, 128)))


def edge_inflow(count, in_ref, coef_ref, edge_ref, flow_ref):
    for pair in range(2):
        both = in_ref[pl.ds(10 + pair, count, stride=BACK), :]
        edge_ref[pair * 2] = both
        edge_ref[pair * 2 + 1] = roll(both, 64, 1)

    def take(k, c, t):
        return coef_ref[k * 4 + c, t : t + 1, :]

    zero = jnp.zeros((1, 128), F32)
    one, two = zero, zero
    sums = []
    for t in range(count):
        flow_ref[0, t : t + 1, :] = one
        flow_ref[1, t : t + 1, :] = two
        made = [edge_ref[k, t : t + 1, :] + take(k, 0, t) * one + take(k, 1, t) * two for k in range(4)]
        one, two = made[:2]
        sums.append(made[2:])
    one, two = zero, zero
    for t in reversed(range(count)):
        flow_ref[2, t : t + 1, :] = one
        flow_ref[3, t : t + 1, :] = two
        one, two = [sums[t][k - 2] + take(k, 2, t) * one + take(k, 3, t) * two for k in (2, 3)]


def final_kernel(
    cells, count, f_ref, in_ref, edge_coef_ref, coef_ref, cons_mat, out_hbm, shift_ref, edge_ref, flow_ref, made_ref, sems
):
    sub, lane = iotas()
    edge_inflow(count, in_ref, edge_coef_ref, edge_ref, flow_ref)
    place = lax.axis_index("sec")
    outside = outer(sub, lane)
    inflow = gathered(in_ref, 0, lane)
    for k in range(4):
        row = jnp.broadcast_to(flow_ref[k, pl.ds(place, 1), :], TILE)
        for u in range(5):
            value = jnp.sum(jnp.where(lane == u * 8 + sub, row, 0.0), axis=1, keepdims=True)
            inflow[k][u] = inflow[k][u] + jnp.where(outside, value, 0.0)
    added = gathered(in_ref, 5, lane)

    def forward(i, carry, right=None):
        one, two = carry
        new = []
        for n, s in enumerate(SYSTEM):
            value = -(coef_ref[s * 5 + 1, i] * two[n]) - coef_ref[s * 5, i] * one[n]
            if right is not None:
                value = value + coef_ref[s * 5 + 2, i] * right[n]
            shift_ref[n, layer_at(i), :] = f_ref[n, layer_at(i), :] + value
            new.append(value)
        return new, one

    last = (inflow[0], inflow[1])
    for i in (0, 1):
        last = forward(i, last, added[i])
    last = lax.fori_loop(2, cells - 2, forward, last, unroll=7)
    for i in (0, 1):
        last = forward(cells - 2 + i, last, added[2 + i])

    def backward(step, carry):
        i = cells - 1 - step
        one, two = carry
        new = [
            shift_ref[n, layer_at(i), :] - coef_ref[s * 5 + 4, i] * two[n] - coef_ref[s * 5 + 3, i] * one[n]
            for n, s in enumerate(SYSTEM)
        ]
        for n in range(5):
            made_ref[n, layer_at(i), :] = sum(cons_mat[n, v] * new[v] for v in range(5))
        return new, one

    carry = (inflow[2], inflow[3])
    part = cells // STORES
    copies = []
    for p in range(STORES):
        carry = lax.fori_loop(p * part, (p + 1) * part, backward, carry, unroll=part)
        at = pl.ds((cells - (p + 1) * part) * 8, part * 8)
        copies.append(pltpu.make_async_copy(made_ref.at[:, at], out_hbm.at[:, at], sems.at[p]))
        copies[-1].start()
    for copy in copies:
        copy.wait()


def shaped(*shape):
    return jax.ShapeDtypeStruct(shape, F32)


def kept(*shape):
    return pltpu.VMEM(shape, F32)


def near(x):
    return pltpu.with_memory_space_constraint(x, pltpu.VMEM)


def exchanged(x, count):
    chunks = x.reshape(count, 1, x.size // count)
    return lax.all_to_all(chunks, "sec", 0, 0, tiled=True).reshape(x.shape)


def near_scalars(x):
    return pltpu.with_memory_space_constraint(x, pltpu.SMEM)


VMEM = pl.BlockSpec(memory_space=pltpu.VMEM)
SMEM = pl.BlockSpec(memory_space=pltpu.SMEM)
ANY = pl.BlockSpec(memory_space=pl.ANY)


def on_device(state, time_step, to_char, to_cons, lower_bands, upper_bands):
    cells = state.shape[1]
    count = lax.axis_size("sec")
    columns = lax.axis_size("cross")
    flat = state.reshape(5, cells, 4, 2, 128).transpose(0, 1, 3, 2, 4).reshape(5, cells * 8, 128)
    steps = time_step.reshape(cells, 4, 2, 128).transpose(0, 2, 1, 3).reshape(cells * 8, 128)
    block = (5, cells * 8, 128)
    ends, swept, padded, steps, coef, char_mat, cons_mat = pl.pallas_call(
        lambda *refs: own_kernel(cells, *refs),
        out_shape=(
            shaped(count * OUT, 128),
            kept(*block),
            kept(5, (cells + 4) * 8, 128),
            kept(cells * 8, 128),
            pltpu.SMEM((16, 128), F32),
            pltpu.SMEM((5, 5), F32),
            pltpu.SMEM((5, 5), F32),
        ),
        in_specs=[ANY] * 6,
        out_specs=(VMEM,) * 4 + (SMEM,) * 3,
        scratch_shapes=[
            pltpu.VMEM(block, F32),
            pltpu.VMEM((3, cells * 8, 128), F32),
            pltpu.VMEM(lower_bands.shape, F32),
            pltpu.VMEM(upper_bands.shape, F32),
            pltpu.VMEM((16, 128), F32),
            pltpu.SemaphoreType.DMA((PARTS,)),
            pltpu.SemaphoreType.DMA((6,)),
        ],
        name="own",
    )(flat, steps, lower_bands, upper_bands, to_char, to_cons)
    coef, char_mat, cons_mat = near_scalars(coef), near_scalars(char_mat), near_scalars(cons_mat)
    ends = exchanged(ends, count)
    edge, step_edge = pl.pallas_call(
        lambda *refs: edges_kernel(cells, *refs),
        out_shape=(kept(40, 128), kept(*TILE)),
        in_specs=[VMEM] * 2,
        out_specs=(VMEM, VMEM),
        name="edges",
    )(near(padded), near(steps))
    right = [(i, i + 1) for i in range(columns - 1)]
    west = near(lax.ppermute(edge, "cross", right))
    east = near(lax.ppermute(edge, "cross", [(j, i) for i, j in right]))
    inflow, edge_coef, swept = pl.pallas_call(
        lambda *refs: reduced_kernel(cells, count, *refs),
        out_shape=(kept(count * BACK, 128), kept(16, count, 128), kept(*block)),
        in_specs=[VMEM] * 5 + [SMEM] * 2,
        out_specs=(VMEM,) * 3,
        scratch_shapes=[
            pltpu.VMEM((4, 2, count, 128), F32),
            pltpu.VMEM((16, 2, count, 128), F32),
            pltpu.VMEM((4, count, 128), F32),
            pltpu.VMEM(block, F32),
        ],
        name="reduced",
    )(near(ends), near(swept), near(step_edge), west, east, coef, char_mat)
    inflow = exchanged(inflow, count)
    result = pl.pallas_call(
        lambda *refs: final_kernel(cells, count, *refs),
        out_shape=shaped(*block),
        in_specs=[VMEM] * 3 + [SMEM] * 2,
        out_specs=ANY,
        scratch_shapes=[
            pltpu.VMEM(block, F32),
            pltpu.VMEM((4, count, 128), F32),
            pltpu.VMEM((4, count, 128), F32),
            pltpu.VMEM(block, F32),
            pltpu.SemaphoreType.DMA((STORES,)),
        ],
        name="final",
    )(near(swept), near(inflow), near(edge_coef), coef, cons_mat)
    return result.reshape(5, cells, 2, 4, 128).transpose(0, 1, 3, 2, 4).reshape(state.shape)


def solution(mesh):
    in_specs = (
        P(None, "sec", None, "cross"),
        P("sec", None, "cross"),
        P(),
        P(),
        P(None, None, "sec"),
        P(None, None, "sec"),
    )
    out_specs = P(None, "sec", None, "cross")
    return jax.shard_map(
        on_device, mesh=mesh, in_specs=in_specs, out_specs=out_specs, check_vma=False
    )
```

```python
import jax
import jax.numpy as jnp
from jax import lax
from jax.experimental import pallas as pl
from jax.experimental.pallas import tpu as pltpu
from jax.sharding import PartitionSpec as P

SYSTEM = (0, 0, 0, 1, 2)
F32 = jnp.float32
OUT = 12
BACK = 12
PARTS = 2
STORES = 4
UNROLL = 32
TILE = (8, 128)


def iotas():
    sub = lax.broadcasted_iota(jnp.int32, TILE, 0)
    lane = lax.broadcasted_iota(jnp.int32, TILE, 1)
    return sub, lane


def roll(x, shift, axis):
    size = x.shape[axis]
    return pltpu.roll(x, shift % size if isinstance(shift, int) else shift, axis)


def primitives(q):
    inv = 1.0 / jnp.where(q[0] == 0.0, 1.0, q[0])
    kinetic = 0.5 * (q[1] * q[1] + q[2] * q[2] + q[3] * q[3]) * inv
    return inv, 0.4 * (q[4] - kinetic)


def flux(q, inv, pressure, k):
    velocity = q[1 + k] * inv
    parts = [q[1 + k], q[1] * velocity, q[2] * velocity, q[3] * velocity, (q[4] + pressure) * velocity]
    parts[1 + k] = parts[1 + k] + pressure
    return parts


def quarter_move(x, a, b):
    return x if a == b else roll(x, 32 * (b - a), 1)


def by_quarter(lane, xs):
    return jnp.where(
        lane < 64, jnp.where(lane < 32, xs[0], xs[1]), jnp.where(lane < 96, xs[2], xs[3])
    )


def packed_edges(cells, layer):
    sub, lane = iotas()
    total = jnp.zeros(TILE, F32)
    for i in range(cells):
        moved = roll(layer(i), i, 1) if i else layer(i)
        total = jnp.where(lane == jnp.where(sub < 4, i, (i - 1) % 128), moved, total)
    return total


def edges_kernel(cells, x_ref, dt_ref, east_ref, west_ref, dt_edge_ref):
    sub, _ = iotas()
    packed = []
    for v in range(5):
        total = packed_edges(cells, lambda i, v=v: x_ref[v, pl.ds(16 + i * 8, 8), :])
        total = roll(total, 4, 0)
        packed.append(jnp.where(sub < 4, roll(total, 1, 1), roll(total, 127, 1)))
    inv, pressure = primitives(packed)
    parts = flux(packed, inv, pressure, 1)
    for n in range(3):
        one, two = parts[2 * n], parts[min(2 * n + 1, 4)]
        east_ref[pl.ds(n * 8, 8), :] = jnp.where(sub < 4, one, roll(two, 4, 0))
        west_ref[pl.ds(n * 8, 8), :] = jnp.where(sub < 4, roll(two, 4, 0), one)
    dt_edge_ref[...] = packed_edges(cells, lambda i: dt_ref[pl.ds(i * 8, 8), :])


def halved(ref, v):
    pair = ref[pl.ds(v // 2 * 8, 8), :]
    return roll(pair, 4, 0) if v % 2 else pair


def layer_at(i):
    return pl.ds(i * 8 if isinstance(i, int) else pl.multiple_of(i * 8, 8), 8)


def to_char(char_mat, right):
    return [sum(char_mat[u, v] * right[v] for v in range(5)) for u in range(5)]


def spread(out_ref, row, lane, groups):
    for quarter in range(4):
        for k, four in enumerate(groups):
            out_ref[pl.ds(quarter * 8 * OUT + row + k, 8, stride=OUT), :] = by_quarter(
                lane, [quarter_move(four[u], quarter, u) for u in range(4)]
            )


def with_fifth(values):
    return [values[k][:4] for k in range(4)] + [[values[k][4] for k in range(4)]]


def gathered(in_ref, row, lane):
    values = []
    for k in range(5):
        parts = [in_ref[pl.ds(q * 8 * BACK + row + k, 8, stride=BACK), :] for q in range(4)]
        values.append(
            [by_quarter(lane, [quarter_move(parts[q], u, q) for q in range(4)]) for u in range(4)]
        )
    return [values[k] + [values[4][k]] for k in range(4)]


def outer(sub, lane):
    return (lane == jnp.where(sub < 4, 0, 127)) & (sub >= 0)


def swept_back(cells, f_ref, coef_ref):
    def backward(step, carry):
        i = cells - 1 - step
        one, two = carry
        new = [
            f_ref[n, layer_at(i), :] - coef_ref[s * 5 + 4, i] * two[n] - coef_ref[s * 5 + 3, i] * one[n]
            for n, s in enumerate(SYSTEM)
        ]
        return new, one

    return backward


def own_kernel(
    cells, x_hbm, dt_hbm, lower_hbm, upper_hbm, char_hbm, cons_hbm,
    out_ref, f_ref, x_ref, dt_ref, coef_ref, char_mat, cons_mat,
    char_ref, answer_ref, lower_ref, upper_ref, made_ref, x_sems, sems,
):
    sub, lane = iotas()
    rows = cells * 8
    part = rows // PARTS
    x_copies = [
        pltpu.make_async_copy(
            x_hbm.at[:, pl.ds(n * part, part)], x_ref.at[:, pl.ds(16 + n * part, part)], x_sems.at[n]
        )
        for n in range(PARTS)
    ]
    pairs = (
        (lower_hbm, lower_ref),
        (upper_hbm, upper_ref),
        (dt_hbm, dt_ref),
        (char_hbm, char_mat),
        (cons_hbm, cons_mat),
    )
    copies = [pltpu.make_async_copy(a, b, sems.at[n]) for n, (a, b) in enumerate(pairs)]
    for copy in copies[:2] + x_copies[:1] + copies[2:4] + x_copies[1:] + copies[4:]:
        copy.start()
    for v in range(5):
        x_ref[v, 0:16] = jnp.zeros((16, 128), F32)
        x_ref[v, pl.ds(16 + rows, 16)] = jnp.zeros((16, 128), F32)
    made_ref[...] = jnp.zeros(made_ref.shape, F32)
    copies[0].wait()
    copies[1].wait()
    for s in range(3):
        inverse = 1.0 / lower_ref[s, 2:3, :]
        made_ref[s * 5 : s * 5 + 1, 0:cells] = lower_ref[s, 1:2, :] * inverse
        made_ref[s * 5 + 1 : s * 5 + 2, 0:cells] = lower_ref[s, 0:1, :] * inverse
        made_ref[s * 5 + 2 : s * 5 + 3, 0:cells] = inverse
        made_ref[s * 5 + 3 : s * 5 + 5, 0:cells] = upper_ref[s]
    made = pltpu.make_async_copy(made_ref, coef_ref, sems.at[5])
    made.start()
    copies[2].wait()
    copies[3].wait()

    third = sub % 4

    def layer(i):
        return [x_ref[v, layer_at(i + 2), :] for v in range(5)]

    def line(i):
        q = layer(i)
        inv, pressure = primitives(q)
        return flux(q, inv, pressure, 0), inv, pressure

    def cell(i, carry):
        flux_before, (flux_now, inv, pressure) = carry
        q = layer(i)
        flux_after, inv_after, pressure_after = line(i + 1)
        side = flux(q, inv, pressure, 1)
        over = flux(q, inv, pressure, 2)
        two, one, next_one, next_two = (layer(i + n) for n in (-2, -1, 1, 2))
        scale = -0.5 * dt_ref[layer_at(i), :]
        right = []
        for v in range(5):
            down, up = roll(side[v], 1, 1), roll(side[v], 127, 1)
            cut = roll(jnp.where(lane == 0, down, up), 4, 0)
            cut = jnp.where((lane == 0) == (sub < 4), 0.0, cut)
            side_diff = jnp.where(lane == 127, cut, up) - jnp.where(lane == 0, cut, down)
            over_diff = jnp.where(third == 3, roll(over[v], 3, 0), roll(over[v], 7, 0)) - jnp.where(
                third == 0, roll(over[v], 5, 0), roll(over[v], 1, 0)
            )
            fourth = (two[v] + next_two[v]) - 4.0 * (one[v] + next_one[v]) + 6.0 * q[v]
            total = (flux_after[v] - flux_before[v]) + side_diff + over_diff + 0.125 * fourth
            right.append(scale * total)
        for u, value in enumerate(to_char(char_mat, right)):
            char_ref[u, layer_at(i), :] = value
        return flux_now, (flux_after, inv_after, pressure_after)

    begin = 0
    for n in range(PARTS):
        x_copies[n].wait()
        if n == 0:
            carry = (line(-1)[0], line(0))
        end = cells if n == PARTS - 1 else (n + 1) * cells // PARTS - 2
        carry = lax.fori_loop(begin, end, cell, carry, unroll=end - begin)
        begin = end
    copies[4].wait()
    made.wait()
    top, bottom = line(0), line(cells - 1)
    first_two, last_two = (layer(0), layer(1)), (layer(cells - 2), layer(cells - 1))
    gives = (
        [0.125 * (last_two[0][v] - 4.0 * last_two[1][v]) - bottom[0][v] for v in range(5)],
        [0.125 * last_two[1][v] for v in range(5)],
        [0.125 * first_two[0][v] for v in range(5)],
        [0.125 * (first_two[1][v] - 4.0 * first_two[0][v]) + top[0][v] for v in range(5)],
    )
    gives = [to_char(char_mat, give) for give in gives]

    unit = [jnp.where((lane == n) & (sub >= 0), 1.0, 0.0).astype(F32) for n in range(8)]
    zero = jnp.where((lane < 0) & (sub < 0), 1.0, 0.0).astype(F32)

    def forward(i, carry, right=None):
        one, two = carry
        new = []
        for n, s in enumerate(SYSTEM + (0, 1, 2)):
            value = -(coef_ref[s * 5 + 1, i] * two[n])
            if n < 5:
                value = coef_ref[s * 5 + 2, i] * char_ref[n, layer_at(i), :] + value
            elif right is not None:
                value = coef_ref[s * 5 + 2, i] * right + value
            value = value - coef_ref[s * 5, i] * one[n]
            if n < 5:
                f_ref[n, layer_at(i), :] = value
            else:
                answer_ref[n - 5, layer_at(i), :] = value
            new.append(value)
        return new, one

    def backward(step, carry):
        i = cells - 1 - step
        one, two = carry
        new = []
        for n, s in enumerate(SYSTEM + (0, 1, 2)):
            value = f_ref[n, layer_at(i), :] if n < 5 else answer_ref[n - 5, layer_at(i), :]
            new.append(value - coef_ref[s * 5 + 4, i] * two[n] - coef_ref[s * 5 + 3, i] * one[n])
        return new, one

    start = [zero] * 5
    last = (start + [unit[0]] * 3, start + [unit[1]] * 3)
    for i in (0, 1):
        last = forward(i, last, unit[4 + i])
    last = lax.fori_loop(2, cells - 2, forward, last, unroll=cells - 4)
    for i in (0, 1):
        last = forward(cells - 2 + i, last, unit[6 + i])
    first = lax.fori_loop(0, cells, backward, (start + [unit[2]] * 3, start + [unit[3]] * 3), unroll=UNROLL)
    ends = last + first
    response = jnp.zeros(TILE, F32)
    for s in range(3):
        for k in range(4):
            at = (s * 4 + k) * 8
            moved = ends[k][5 + s] if at == 0 else roll(ends[k][5 + s], at, 1)
            response = jnp.where((lane >= at) & (lane < at + 8), moved, response)
    response = jnp.broadcast_to(response[0:1, :], TILE)
    spread(out_ref, 0, lane, with_fifth(ends))
    spread(out_ref, 6, lane, with_fifth(gives))
    spread(out_ref, 11, lane, [[-0.5 * dt_ref[pl.ds(i * 8, 8), :] for i in (0, 1, cells - 2, cells - 1)]])
    for quarter in range(4):
        out_ref[pl.ds(quarter * 8 * OUT + 5, 8, stride=OUT), :] = response


def reduced_kernel(
    cells, count, in_ref, f_in, dt_edge_ref, east_ref, west_ref, scalars, char_mat,
    out_ref, edge_coef_ref, f_ref, part_ref, coef_ref, four_ref, sweep_ref,
):
    lane = lax.broadcasted_iota(jnp.int32, (count, 128), 1)
    place = lax.broadcasted_iota(jnp.int32, (count, 128), 0)

    def rows(n):
        return in_ref[pl.ds(n, count, stride=OUT), :]

    def put(n, value):
        out_ref[pl.ds(n, count, stride=BACK), :] = value

    response = rows(5)

    def wide(k, c):
        at = [(s * 4 + k) * 8 + c for s in range(3)]
        return [jnp.broadcast_to(response[:, n : n + 1], (count, 128)) for n in at]

    def factor(systems):
        return jnp.where(lane < 96, systems[0], systems[1]), systems[2]

    step, fifth = rows(11), rows(10)
    added = []
    for m in range(4):
        scales = by_quarter(lane, [quarter_move(step, m, u) for u in range(4)])
        pair = []
        for give, scale in ((rows(6 + m), scales), (quarter_move(fifth, m, 0), quarter_move(step, m, 0))):
            if m < 2:
                give = jnp.where(place == 0, 0.0, roll(give, 1, 0))
            else:
                give = jnp.where(place == count - 1, 0.0, roll(give, count - 1, 0))
            pair.append(scale * give)
        added.append(pair)
        put(5 + m, pair[0])
    put(9, by_quarter(lane, [quarter_move(added[m][1], 0, m) for m in range(4)]))
    fifth = rows(4)
    for k in range(4):
        values = [rows(k), quarter_move(fifth, k, 0)]
        for m in range(4):
            for tile, part in enumerate(factor(wide(k, 4 + m))):
                values[tile] = values[tile] + part * added[m][tile]
        for tile in range(2):
            part_ref[k, tile] = values[tile]
        for c in range(2 if k < 2 else 4):
            systems = wide(k, c)
            for tile, part in enumerate(factor(systems)):
                coef_ref[k * 4 + c, tile] = part
            edge_coef_ref[k * 4 + c] = jnp.where(
                lane < 24, systems[0], jnp.where(lane < 32, systems[1], systems[2])
            )
    sub, tile_lane = iotas()
    scale = -0.5 * dt_edge_ref[...]
    beside = to_char(
        char_mat,
        [
            scale * jnp.where(sub < 4, -halved(west_ref, v), halved(east_ref, v))
            for v in range(5)
        ],
    )
    outside = outer(sub, tile_lane)

    def forward(i, carry):
        one, two = carry
        new = []
        for n, s in enumerate(SYSTEM):
            char = jnp.where(outside, roll(beside[n], (128 - i) % 128, 1), 0.0)
            value = scalars[s * 5 + 2, i] * char - scalars[s * 5 + 1, i] * two[n] - scalars[s * 5, i] * one[n]
            sweep_ref[n, layer_at(i), :] = value
            f_ref[n, layer_at(i), :] = f_in[n, layer_at(i), :] + value
            new.append(value)
        return new, one

    backward = swept_back(cells, sweep_ref, scalars)
    blank = jnp.zeros(TILE, F32)
    zero = jnp.zeros((1, 128), F32)

    def take(ref, n, tile, t):
        return ref[n, tile, t : t + 1, :]

    inflow = [(zero, zero), (zero, zero)]
    sums = []
    last = ([blank] * 5, [blank] * 5)
    for t in range(count):
        for i in range(t * cells // count, (t + 1) * cells // count):
            last = forward(i, last)
        row = []
        for tile in range(2):
            one, two = inflow[tile]
            for k, value in ((0, one), (1, two)):
                if tile == 0:
                    out_ref[t * BACK + k : t * BACK + k + 1, :] = value
                else:
                    four_ref[k, t : t + 1, :] = value
            made = [
                take(part_ref, k, tile, t)
                + take(coef_ref, k * 4, tile, t) * one
                + take(coef_ref, k * 4 + 1, tile, t) * two
                for k in range(4)
            ]
            inflow[tile] = (made[0], made[1])
            row.append((made[2], made[3]))
        sums.append(row)
    inflow = [(zero, zero), (zero, zero)]
    first = ([blank] * 5, [blank] * 5)
    for t in reversed(range(count)):
        for i in reversed(range(t * cells // count, (t + 1) * cells // count)):
            first = backward(cells - 1 - i, first)
        for tile in range(2):
            one, two = inflow[tile]
            for k, value in ((2, one), (3, two)):
                if tile == 0:
                    out_ref[t * BACK + k : t * BACK + k + 1, :] = value
                else:
                    four_ref[k, t : t + 1, :] = value
            inflow[tile] = tuple(
                sums[t][tile][k - 2]
                + take(coef_ref, k * 4 + 2, tile, t) * one
                + take(coef_ref, k * 4 + 3, tile, t) * two
                for k in (2, 3)
            )
    put(4, by_quarter(lane, [quarter_move(four_ref[k], 0, k) for k in range(4)]))
    ends = last + first
    for pair in range(2):
        total = blank
        for n in range(2):
            for u in range(5):
                value = jnp.sum(ends[pair * 2 + n][u], axis=1, keepdims=True)
                total = jnp.where(tile_lane == n * 64 + u * 8 + sub, value, total)
        put(10 + pair, jnp.broadcast_to(jnp.sum(total, axis=0, keepdims=True), (count, 128)))


def edge_inflow(count, in_ref, coef_ref, edge_ref, flow_ref):
    for pair in range(2):
        both = in_ref[pl.ds(10 + pair, count, stride=BACK), :]
        edge_ref[pair * 2] = both
        edge_ref[pair * 2 + 1] = roll(both, 64, 1)

    def take(k, c, t):
        return coef_ref[k * 4 + c, t : t + 1, :]

    zero = jnp.zeros((1, 128), F32)
    one, two = zero, zero
    sums = []
    for t in range(count):
        flow_ref[0, t : t + 1, :] = one
        flow_ref[1, t : t + 1, :] = two
        made = [edge_ref[k, t : t + 1, :] + take(k, 0, t) * one + take(k, 1, t) * two for k in range(4)]
        one, two = made[:2]
        sums.append(made[2:])
    one, two = zero, zero
    for t in reversed(range(count)):
        flow_ref[2, t : t + 1, :] = one
        flow_ref[3, t : t + 1, :] = two
        one, two = [sums[t][k - 2] + take(k, 2, t) * one + take(k, 3, t) * two for k in (2, 3)]


def final_kernel(
    cells, count, f_ref, in_ref, edge_coef_ref, coef_ref, cons_mat, out_hbm, shift_ref, edge_ref, flow_ref, made_ref, sems
):
    sub, lane = iotas()
    edge_inflow(count, in_ref, edge_coef_ref, edge_ref, flow_ref)
    place = lax.axis_index("sec")
    outside = outer(sub, lane)
    inflow = gathered(in_ref, 0, lane)
    for k in range(4):
        row = jnp.broadcast_to(flow_ref[k, pl.ds(place, 1), :], TILE)
        for u in range(5):
            value = jnp.sum(jnp.where(lane == u * 8 + sub, row, 0.0), axis=1, keepdims=True)
            inflow[k][u] = inflow[k][u] + jnp.where(outside, value, 0.0)
    added = gathered(in_ref, 5, lane)

    def forward(i, carry, right=None):
        one, two = carry
        new = []
        for n, s in enumerate(SYSTEM):
            value = -(coef_ref[s * 5 + 1, i] * two[n]) - coef_ref[s * 5, i] * one[n]
            if right is not None:
                value = value + coef_ref[s * 5 + 2, i] * right[n]
            shift_ref[n, layer_at(i), :] = f_ref[n, layer_at(i), :] + value
            new.append(value)
        return new, one

    last = (inflow[0], inflow[1])
    for i in (0, 1):
        last = forward(i, last, added[i])
    last = lax.fori_loop(2, cells - 2, forward, last, unroll=7)
    for i in (0, 1):
        last = forward(cells - 2 + i, last, added[2 + i])

    def backward(step, carry):
        i = cells - 1 - step
        one, two = carry
        new = [
            shift_ref[n, layer_at(i), :] - coef_ref[s * 5 + 4, i] * two[n] - coef_ref[s * 5 + 3, i] * one[n]
            for n, s in enumerate(SYSTEM)
        ]
        for n in range(5):
            made_ref[n, layer_at(i), :] = sum(cons_mat[n, v] * new[v] for v in range(5))
        return new, one

    carry = (inflow[2], inflow[3])
    part = cells // STORES
    copies = []
    for p in range(STORES):
        carry = lax.fori_loop(p * part, (p + 1) * part, backward, carry, unroll=part)
        at = pl.ds((cells - (p + 1) * part) * 8, part * 8)
        copies.append(pltpu.make_async_copy(made_ref.at[:, at], out_hbm.at[:, at], sems.at[p]))
        copies[-1].start()
    for copy in copies:
        copy.wait()


def shaped(*shape):
    return jax.ShapeDtypeStruct(shape, F32)


def kept(*shape):
    return pltpu.VMEM(shape, F32)


def near(x):
    return pltpu.with_memory_space_constraint(x, pltpu.VMEM)


def exchanged(x, count):
    chunks = x.reshape(count, 1, x.size // count)
    return lax.all_to_all(chunks, "sec", 0, 0, tiled=True).reshape(x.shape)


def near_scalars(x):
    return pltpu.with_memory_space_constraint(x, pltpu.SMEM)


VMEM = pl.BlockSpec(memory_space=pltpu.VMEM)
SMEM = pl.BlockSpec(memory_space=pltpu.SMEM)
ANY = pl.BlockSpec(memory_space=pl.ANY)


def on_device(state, time_step, to_char, to_cons, lower_bands, upper_bands):
    cells = state.shape[1]
    count = lax.axis_size("sec")
    columns = lax.axis_size("cross")
    flat = state.reshape(5, cells, 4, 2, 128).transpose(0, 1, 3, 2, 4).reshape(5, cells * 8, 128)
    steps = time_step.reshape(cells, 4, 2, 128).transpose(0, 2, 1, 3).reshape(cells * 8, 128)
    block = (5, cells * 8, 128)
    ends, swept, padded, steps, coef, char_mat, cons_mat = pl.pallas_call(
        lambda *refs: own_kernel(cells, *refs),
        out_shape=(
            shaped(count * OUT, 128),
            kept(*block),
            kept(5, (cells + 4) * 8, 128),
            kept(cells * 8, 128),
            pltpu.SMEM((16, 128), F32),
            pltpu.SMEM((5, 5), F32),
            pltpu.SMEM((5, 5), F32),
        ),
        in_specs=[ANY] * 6,
        out_specs=(VMEM,) * 4 + (SMEM,) * 3,
        scratch_shapes=[
            pltpu.VMEM(block, F32),
            pltpu.VMEM((3, cells * 8, 128), F32),
            pltpu.VMEM(lower_bands.shape, F32),
            pltpu.VMEM(upper_bands.shape, F32),
            pltpu.VMEM((16, 128), F32),
            pltpu.SemaphoreType.DMA((PARTS,)),
            pltpu.SemaphoreType.DMA((6,)),
        ],
        name="own",
    )(flat, steps, lower_bands, upper_bands, to_char, to_cons)
    coef, char_mat, cons_mat = near_scalars(coef), near_scalars(char_mat), near_scalars(cons_mat)
    ends = exchanged(ends, count)
    to_east, to_west, step_edge = pl.pallas_call(
        lambda *refs: edges_kernel(cells, *refs),
        out_shape=(kept(24, 128), kept(24, 128), kept(*TILE)),
        in_specs=[VMEM] * 2,
        out_specs=(VMEM,) * 3,
        name="edges",
    )(near(padded), near(steps))
    right = [(i, i + 1) for i in range(columns - 1)]
    west = near(lax.ppermute(to_east, "cross", right))
    east = near(lax.ppermute(to_west, "cross", [(j, i) for i, j in right]))
    inflow, edge_coef, swept = pl.pallas_call(
        lambda *refs: reduced_kernel(cells, count, *refs),
        out_shape=(kept(count * BACK, 128), kept(16, count, 128), kept(*block)),
        in_specs=[VMEM] * 5 + [SMEM] * 2,
        out_specs=(VMEM,) * 3,
        scratch_shapes=[
            pltpu.VMEM((4, 2, count, 128), F32),
            pltpu.VMEM((16, 2, count, 128), F32),
            pltpu.VMEM((4, count, 128), F32),
            pltpu.VMEM(block, F32),
        ],
        name="reduced",
    )(near(ends), near(swept), near(step_edge), east, west, coef, char_mat)
    inflow = exchanged(inflow, count)
    result = pl.pallas_call(
        lambda *refs: final_kernel(cells, count, *refs),
        out_shape=shaped(*block),
        in_specs=[VMEM] * 3 + [SMEM] * 2,
        out_specs=ANY,
        scratch_shapes=[
            pltpu.VMEM(block, F32),
            pltpu.VMEM((4, count, 128), F32),
            pltpu.VMEM((4, count, 128), F32),
            pltpu.VMEM(block, F32),
            pltpu.SemaphoreType.DMA((STORES,)),
        ],
        name="final",
    )(near(swept), near(inflow), near(edge_coef), coef, cons_mat)
    return result.reshape(5, cells, 2, 4, 128).transpose(0, 1, 3, 2, 4).reshape(state.shape)


def solution(mesh):
    in_specs = (
        P(None, "sec", None, "cross"),
        P("sec", None, "cross"),
        P(),
        P(),
        P(None, None, "sec"),
        P(None, None, "sec"),
    )
    out_specs = P(None, "sec", None, "cross")
    return jax.shard_map(
        on_device, mesh=mesh, in_specs=in_specs, out_specs=out_specs, check_vma=False
    )
```
